256 devices in a mesh: guide: 2 (over core), seq: 32 (over x, z), rep: 4 (over y).
Axes of the slice: x: 4, y: 4, z: 8, core: 2. Of those that a mesh axis runs over, the one named last changes fastest.
Arguments:
- queries: bfloat16 [2, 16384, 4096], P('guide', ('seq', 'rep')), may hold values from -12 to 12
- key_vectors: bfloat16 [2, 16384, 4096], P('guide', ('seq', 'rep')), may hold values from -12 to 12
- value_vectors: bfloat16 [2, 16384, 4096], P('guide', ('seq', 'rep')), may hold values from -6 to 6
- cluster_order: int32 [32, 16384], P('seq'), may hold values from 0 to 16383, as said below
- key_blocks: int32 [32, 64, 8], P('seq'), may hold values from 0 to 63, as said below
- extents: int32 [32, 64], P('seq'), may hold values from 1 to 8, as said below
Outputs:
- guided: bfloat16 [16384, 4096], P(('seq', 'rep'), 'guide')
The draws below stay inside these ranges and needn't reach their ends.
Inputs may be any that keep to these rules, and one draw needn't show every extreme that they name: `cluster_order`: each row is a permutation of the 16384 tokens. Entry 0 of key_blocks[h, c] is c itself, and the entries of one row are distinct. Only the first extents[h, c] entries of key_blocks[h, c] are listed; the value 8 occurs in every draw.
All inputs are finite; a program needn't handle non-finite values.
Results may differ from the reference program's by a relative error of at most 0.0057.
Values may be sent and summed in bfloat16 or wider, within the bound.
A program may use at most 128 MiB of HBM per device.

```python
import jax
import jax.numpy as jnp
from jax import lax

HEADS = 32
HEAD_DIM = 128
CLUSTER = 256
MAX_BLOCKS = 8
TOKENS = 16384
CLUSTERS = 64
WIDTH = 4096


def shared_order(key):
    row_keys = jax.random.split(jax.random.fold_in(key, 101), HEADS)
    return jax.vmap(lambda single: jax.random.permutation(single, TOKENS))(row_keys).astype(jnp.int32)


def draw_queries(key, part):
    key = jax.random.fold_in(key, 1)
    drawn = 2.0 * jax.random.normal(key, (2, TOKENS, HEADS * HEAD_DIM), jnp.float32)
    return jnp.clip(drawn, -12.0, 12.0).astype(jnp.bfloat16)


def draw_key_vectors(key, part):
    key = jax.random.fold_in(key, 2)
    drawn = jax.random.normal(key, (2, TOKENS, HEADS * HEAD_DIM), jnp.float32)
    return jnp.clip(drawn, -12.0, 12.0).astype(jnp.bfloat16)


def draw_cluster_order(key, part):
    return shared_order(key)


def draw_key_blocks(key, part):
    key = jax.random.fold_in(key, 3)
    row_keys = jax.random.split(key, HEADS * CLUSTERS)
    others = jax.vmap(lambda single: jax.random.permutation(single, CLUSTERS - 1))(row_keys)[:, :MAX_BLOCKS - 1]
    own_cluster = jnp.tile(jnp.arange(CLUSTERS, dtype=jnp.int32), HEADS)
    others = others.astype(jnp.int32)
    others = others + (others >= own_cluster[:, None]).astype(jnp.int32)
    listed = jnp.concatenate([own_cluster[:, None], others], axis=1)
    return listed.reshape(HEADS, CLUSTERS, MAX_BLOCKS).astype(jnp.int32)


def draw_extents(key, part):
    key = jax.random.fold_in(key, 4)
    level_key, busy_key, count_key, spot_key = jax.random.split(key, 4)
    head_level = jax.random.randint(level_key, (HEADS,), 0, 4)
    head_cap = jnp.where(head_level == 3, MAX_BLOCKS, jnp.where(head_level == 2, min(2, MAX_BLOCKS), 1))
    busiest = jax.random.randint(busy_key, (), 0, HEADS)
    head_cap = head_cap.at[busiest].set(MAX_BLOCKS)
    counts = jax.random.randint(count_key, (HEADS, CLUSTERS), 1, head_cap[:, None] + 1)
    busy_spot = jax.random.randint(spot_key, (), 0, CLUSTERS)
    return counts.at[busiest, busy_spot].set(MAX_BLOCKS).astype(jnp.int32)


def block_scale(own_key, shape, shards, least, high):
    factor_of, own = 1.0, jax.random.fold_in(own_key, 6)
    for dim, blocks in shards:
        steps = jnp.exp(jax.random.uniform(jax.random.fold_in(own, dim), (blocks,), jnp.float32, least / len(shards), high / len(shards)))
        factor_of = factor_of * jnp.repeat(steps, shape[dim] // blocks).reshape([-1 if axis == dim else 1 for axis in range(len(shape))])
    return factor_of


def noise(key, dims, deviation, limit, shards=(), held_as=jnp.bfloat16):
    values = jax.random.normal(key, dims, jnp.float32) * deviation
    if len(shards) > 0:
        values = block_scale(key, dims, shards, -0.22, 0.18) * values
    return jnp.clip(values, min=-limit, max=limit).astype(held_as)


def setup_inputs(seed: int = 0) -> dict:
    key_of = jax.random.split(jax.random.key(seed), 7)
    queries = draw_queries(jax.random.fold_in(key_of[6], 71), 0)
    key_vectors = draw_key_vectors(jax.random.fold_in(key_of[6], 71), 0)
    value_vectors = noise(key_of[2], (2, TOKENS, WIDTH), 1.0, 6.0, ((0, 2), (1, 128)))
    cluster_order = draw_cluster_order(jax.random.fold_in(key_of[6], 71), 0)
    key_blocks = draw_key_blocks(jax.random.fold_in(key_of[6], 71), 0)
    extents = draw_extents(jax.random.fold_in(key_of[6], 71), 0)
    return {"queries": queries, "key_vectors": key_vectors, "value_vectors": value_vectors, "cluster_order": cluster_order, "key_blocks": key_blocks, "extents": extents}


GUIDE_SCALE = 5.0


def attend_head(head_queries, head_keys, head_values, token_order, listed, counts):
    sorted_queries = head_queries[token_order].reshape(CLUSTERS, CLUSTER, HEAD_DIM)
    sorted_keys = head_keys[token_order].reshape(CLUSTERS, CLUSTER, HEAD_DIM)
    sorted_values = head_values[token_order].reshape(CLUSTERS, CLUSTER, HEAD_DIM)

    def one_cluster(packed):
        cluster_queries, cluster_list, cluster_count = packed
        block_keys = sorted_keys[cluster_list].reshape(MAX_BLOCKS * CLUSTER, HEAD_DIM)
        block_values = sorted_values[cluster_list].reshape(MAX_BLOCKS * CLUSTER, HEAD_DIM)
        scores = jnp.dot(cluster_queries, block_keys.T, preferred_element_type=jnp.float32) * (HEAD_DIM ** -0.5)
        live_mask = jnp.repeat(jnp.arange(MAX_BLOCKS) < cluster_count, CLUSTER)
        scores = jnp.where(live_mask[None, :], scores, -jnp.inf)
        shifted = jnp.exp(scores - jnp.max(scores, axis=1, keepdims=True))
        weights = (shifted / jnp.sum(shifted, axis=1, keepdims=True)).astype(jnp.bfloat16)
        return jnp.dot(weights, block_values, preferred_element_type=jnp.float32).astype(jnp.bfloat16)

    attended = lax.map(one_cluster, (sorted_queries, listed, counts)).reshape(TOKENS, HEAD_DIM)
    return jnp.zeros_like(head_queries).at[token_order].set(attended)


def head_major(array):
    return array.reshape(TOKENS, HEADS, HEAD_DIM).transpose(1, 0, 2)


def reference(queries, key_vectors, value_vectors, cluster_order, key_blocks, extents):
    branches = []
    for branch in range(2):
        def one_head(packed):
            return attend_head(*packed)

        per_head = lax.map(one_head, (head_major(queries[branch]), head_major(key_vectors[branch]),
                                      head_major(value_vectors[branch]), cluster_order, key_blocks, extents))
        branches.append(per_head.transpose(1, 0, 2).reshape(TOKENS, HEADS * HEAD_DIM))
    conditioned = branches[0].astype(jnp.float32)
    unconditioned = branches[1].astype(jnp.float32)
    return (unconditioned + GUIDE_SCALE * (conditioned - unconditioned)).astype(jnp.bfloat16)
```

```python
import functools

import jax
import jax.numpy as jnp
from jax import lax
from jax.experimental import pallas as pl
from jax.experimental.pallas import tpu as pltpu
from jax.sharding import PartitionSpec as P

MESH = pl.DeviceIdType.MESH
CLUSTER = 256
GUIDE_SCALE = 5.0
HEADS = 32
SEQ_X, SEQ_Z = 4, 8
REPS = 4
TOKENS = 16384
DIM = 128
SPAN = TOKENS // REPS
LOCAL = 128
CLUSTERS = TOKENS // CLUSTER
CHUNK = 512
CHUNKS = SPAN // CHUNK
WINDOW = 128
QROWS = 96
f32, bf16, i32 = jnp.float32, jnp.bfloat16, jnp.int32

NT = (((1,), (1,)), ((), ()))


def dot_nt(a, b):
    return lax.dot_general(a, b, NT, preferred_element_type=f32)


def iota(shape, dim):
    return lax.broadcasted_iota(i32, shape, dim)


def gather_kernel(q_in, k_in, v_in, order_ref, kall, vall, qs, dest_out, destt_out,
                  rx, sorted_, onehot, key_s, low_s, rhi_s, rlo_s, dest_s, destt_s,
                  send_sem, recv_sem, own_sem, ysend, yrecv, out_sem):
    me = lax.axis_index("seq")
    rep = lax.axis_index("rep")
    x, z = me // SEQ_Z, me % SEQ_Z
    right, left = lax.rem(rep + 1, REPS), lax.rem(rep + REPS - 1, REPS)
    ins = (k_in, v_in, q_in)
    alls = (kall, vall)

    def peer_of(off):
        return lax.rem(x + off // SEQ_Z, SEQ_X) * SEQ_Z + lax.rem(z + off % SEQ_Z, SEQ_Z)

    barrier = pltpu.get_barrier_semaphore()

    def greet(off, _):
        pl.semaphore_signal(barrier, inc=1, device_id={"seq": peer_of(off)}, device_id_type=MESH)
        return 0

    lax.fori_loop(1, HEADS, greet, 0)
    pl.semaphore_signal(barrier, inc=1, device_id={"rep": right}, device_id_type=MESH)
    pl.semaphore_signal(barrier, inc=1, device_id={"rep": left}, device_id_type=MESH)
    pl.semaphore_wait(barrier, HEADS - 1 + 2)

    def a2a_copy(a, peer, slot):
        return pltpu.make_async_remote_copy(
            src_ref=ins[a].at[:, pl.ds(pl.multiple_of(peer * DIM, DIM), DIM)],
            dst_ref=rx.at[a, slot],
            send_sem=send_sem.at[a, peer], recv_sem=recv_sem.at[a, slot],
            device_id={"seq": peer}, device_id_type=MESH)

    def own_copy(a):
        return pltpu.make_async_copy(
            ins[a].at[:, pl.ds(pl.multiple_of(me * DIM, DIM), DIM)], rx.at[a, me], own_sem.at[a])

    for a in range(3):
        own_copy(a).start()

        def send(off, _):
            a2a_copy(a, peer_of(off), me).start()
            return 0

        lax.fori_loop(1, HEADS, send, 0)

    order = order_ref[...]
    block = order >> 7
    mine = (block & (REPS - 1)) == rep
    key_s[...] = jnp.where(mine, block >> 2, -1)
    low_s[...] = order & (LOCAL - 1)
    present = jnp.where(mine, 1.0, 0.0).astype(bf16)
    rows, cols = iota((128, 128), 0), iota((128, 128), 1)
    upper = jnp.where(rows < cols, 1.0, 0.0).astype(bf16)
    lower = jnp.where(cols < rows, 1.0, 0.0).astype(bf16)
    ones = jnp.ones((128, 128), bf16)
    within = jnp.dot(present, upper, preferred_element_type=f32)
    totals = jnp.dot(present, ones, preferred_element_type=f32).astype(bf16)
    rank = within + jnp.dot(lower, totals, preferred_element_type=f32)
    rank_hi = jnp.floor(rank * (1.0 / 64.0))
    rhi_s[...] = rank_hi
    rlo_s[...] = rank - 64.0 * rank_hi

    def accumulate(step, carry):
        d, dt = carry
        his, los, bs = [], [], []
        base = pl.multiple_of(step * 8, 8)
        key8, low8 = key_s[pl.ds(base, 8), :], low_s[pl.ds(base, 8), :]
        rhi8, rlo8 = rhi_s[pl.ds(base, 8), :], rlo_s[pl.ds(base, 8), :]
        for j in range(8):
            hit = iota((HEADS, 128), 0) == key8[j:j + 1]
            his.append(jnp.where(hit, rhi8[j:j + 1], 0.0))
            los.append(jnp.where(hit, rlo8[j:j + 1], 0.0))
            bs.append(jnp.where(iota((128, 128), 0) == low8[j:j + 1], 1.0, 0.0))
        left_m = jnp.concatenate([jnp.concatenate(his, 1), jnp.concatenate(los, 1)], 0).astype(bf16)
        right_m = jnp.concatenate(bs, 1).astype(bf16)
        return d + dot_nt(left_m, right_m), dt + dot_nt(right_m, left_m)

    d, dt = lax.fori_loop(0, 16, accumulate, (jnp.zeros((2 * HEADS, 128), f32), jnp.zeros((128, 2 * HEADS), f32)))
    dest_s[...] = (64.0 * d[:HEADS] + d[HEADS:]).astype(i32)
    destt_s[...] = (64.0 * dt[:, :HEADS] + dt[:, HEADS:]).astype(i32)
    dest_copy = pltpu.make_async_copy(dest_s, dest_out, out_sem.at[0])
    destt_copy = pltpu.make_async_copy(destt_s, destt_out, out_sem.at[1])
    dest_copy.start()
    destt_copy.start()

    def build(kb, _):
        base = pl.multiple_of(kb * 256, 256)
        row = iota((256, 128), 0) + base
        for s in range(HEADS):
            onehot[pl.ds(base, 256), s * 128:(s + 1) * 128] = jnp.where(
                row == dest_s[s:s + 1, :], 1.0, 0.0).astype(bf16)
        return 0

    lax.fori_loop(0, SPAN // 256, build, 0)

    def wait_in(a):
        def one(off, _):
            a2a_copy(a, me, peer_of(off)).wait_recv()
            return 0

        lax.fori_loop(1, HEADS, one, 0)
        own_copy(a).wait()

    def rows_of(c):
        return pl.ds(pl.multiple_of(c * CHUNK, CHUNK), CHUNK)

    def ycopy(a, kind, c):
        if kind == 0:
            src, slot, to = sorted_.at[a, rows_of(c)], rep, right
        elif kind == 1:
            src, slot, to = sorted_.at[a, rows_of(c)], rep, left
        else:
            even = lax.rem(c, 2) == 0
            slot = jnp.where(even, left, right)
            to = jnp.where(even, right, left)
            src = alls[a].at[slot, rows_of(c)]
        return pltpu.make_async_remote_copy(
            src_ref=src, dst_ref=alls[a].at[slot, rows_of(c)],
            send_sem=ysend.at[a, kind, c], recv_sem=yrecv.at[a, kind, c],
            device_id={"rep": to}, device_id_type=MESH)

    def keep_copy(a, c):
        to = alls[a].at[rep, rows_of(c)] if a < 2 else qs.at[rows_of(c)]
        return pltpu.make_async_copy(sorted_.at[a, rows_of(c)], to, out_sem.at[2 + a * CHUNKS + c])

    def wait_y(a, kind, c):
        if kind == 0:
            slot = left
        elif kind == 1:
            slot = right
        else:
            slot = lax.rem(rep + 2, REPS)
        pltpu.make_async_remote_copy(
            src_ref=sorted_.at[a, rows_of(c)], dst_ref=alls[a].at[slot, rows_of(c)],
            send_sem=ysend.at[a, kind, c], recv_sem=yrecv.at[a, kind, c],
            device_id={"rep": right}, device_id_type=MESH).wait_recv()

    def forward(a, c):
        wait_y(a, 0, c)
        wait_y(a, 1, c)
        ycopy(a, 2, c).start()

    for a in range(3):
        wait_in(a)

        def sort(c, _):
            sorted_[a, rows_of(c)] = jnp.dot(
                onehot[rows_of(c), :], rx[a].reshape(SPAN, DIM), preferred_element_type=f32).astype(bf16)
            if a < 2:
                ycopy(a, 0, c).start()
                ycopy(a, 1, c).start()
            keep_copy(a, c).start()
            if a > 0:
                forward(a - 1, c)
            return 0

        lax.fori_loop(0, CHUNKS, sort, 0)

    dest_copy.wait()
    destt_copy.wait()

    def finish(c, _):
        for a in range(3):
            keep_copy(a, c).wait()
        for a in range(2):
            wait_y(a, 2, c)
            for kind in range(3):
                ycopy(a, kind, c).wait_send()
        return 0

    lax.fori_loop(0, CHUNKS, finish, 0)

    def sent(off, _):
        for a in range(3):
            a2a_copy(a, peer_of(off), me).wait_send()
        return 0

    lax.fori_loop(1, HEADS, sent, 0)


def gather_call(q, k, v, order):
    any_ = pl.BlockSpec(memory_space=pl.ANY)
    vmem = pl.BlockSpec(memory_space=pltpu.VMEM)
    return pl.pallas_call(
        gather_kernel,
        out_shape=(
            jax.ShapeDtypeStruct((REPS, SPAN, DIM), bf16),
            jax.ShapeDtypeStruct((REPS, SPAN, DIM), bf16),
            jax.ShapeDtypeStruct((SPAN, DIM), bf16),
            jax.ShapeDtypeStruct((HEADS, LOCAL), i32),
            jax.ShapeDtypeStruct((LOCAL, HEADS), i32),
        ),
        in_specs=[any_, any_, any_, vmem],
        out_specs=(any_,) * 5,
        scratch_shapes=[
            pltpu.VMEM((3, HEADS, LOCAL, DIM), bf16),
            pltpu.VMEM((3, SPAN, DIM), bf16),
            pltpu.VMEM((SPAN, SPAN), bf16),
            pltpu.VMEM((128, 128), i32),
            pltpu.VMEM((128, 128), i32),
            pltpu.VMEM((128, 128), f32),
            pltpu.VMEM((128, 128), f32),
            pltpu.VMEM((HEADS, LOCAL), i32),
            pltpu.VMEM((LOCAL, HEADS), i32),
            pltpu.SemaphoreType.DMA((3, HEADS)),
            pltpu.SemaphoreType.DMA((3, HEADS)),
            pltpu.SemaphoreType.DMA((3,)),
            pltpu.SemaphoreType.DMA((2, 3, CHUNKS)),
            pltpu.SemaphoreType.DMA((2, 3, CHUNKS)),
            pltpu.SemaphoreType.DMA((2 + 3 * CHUNKS,)),
        ],
        compiler_params=pltpu.CompilerParams(
            collective_id=0, has_side_effects=True, vmem_limit_bytes=56 * 2**20),
        name="gather_sorted",
    )(q, k, v, order)


def attend_kernel(off_ref, cnt_ref, list_ref, ext_ref, rep_ref, kall, vall, qs, out, kc, vc, acc):
    def piece(c, r, start, k):
        off, n = off_ref[r, c], cnt_ref[r, c]
        lo = (off // 16) * 16 + k * WINDOW
        at = jnp.minimum(lo, SPAN - WINDOW)
        first = jnp.maximum(off, lo)
        last = jnp.minimum(off + n, lo + WINDOW)
        shift = start - off
        m = iota((CLUSTER, WINDOW), 0)
        diff = m - iota((CLUSTER, WINDOW), 1)
        hit = (diff == at + shift) & (m >= first + shift) & (m < last + shift)
        return jnp.where(hit, 1.0, 0.0).astype(bf16), pl.multiple_of(at, 16)

    def compact(c, _):
        start = jnp.int32(0)
        ones, keys, vals = [], [], []
        starts = []
        most = jnp.int32(0)
        for r in range(REPS):
            hot, at = piece(c, r, start, 0)
            ones.append(hot)
            keys.append(kall[r, pl.ds(at, WINDOW), :])
            vals.append(vall[r, pl.ds(at, WINDOW), :])
            starts.append(start)
            start = start + cnt_ref[r, c]
            most = jnp.maximum(most, off_ref[r, c] % 16 + cnt_ref[r, c])
        kv = jnp.concatenate([jnp.concatenate(keys, 0), jnp.concatenate(vals, 0)], 1)
        whole = jnp.dot(jnp.concatenate(ones, 1), kv, preferred_element_type=f32)
        rows = pl.ds(pl.multiple_of(c * CLUSTER, CLUSTER), CLUSTER)
        kc[rows, :] = whole[:, :DIM].astype(bf16)
        vc[rows, :] = whole[:, DIM:].astype(bf16)

        @pl.when(most > WINDOW)
        def _():
            for r in range(REPS):
                def more(k, _):
                    hot, at = piece(c, r, starts[r], k)
                    kc[rows, :] = (kc[rows, :].astype(f32) + jnp.dot(
                        hot, kall[r, pl.ds(at, WINDOW), :], preferred_element_type=f32)).astype(bf16)
                    vc[rows, :] = (vc[rows, :].astype(f32) + jnp.dot(
                        hot, vall[r, pl.ds(at, WINDOW), :], preferred_element_type=f32)).astype(bf16)
                    return 0

                lax.fori_loop(1, 3, more, 0)
        return 0

    lax.fori_loop(0, CLUSTERS, compact, 0)

    rep = rep_ref[0]
    factor = DIM ** -0.5 * 1.4426950408889634

    def attend(c, _):
        off, n, count = off_ref[rep, c], cnt_ref[rep, c], ext_ref[c]
        base = (off // 16) * 16
        windows = jnp.where(n > 0, (off + n - base + QROWS - 1) // QROWS, 0)

        def window(k, _):
            lo = base + k * QROWS
            at = jnp.minimum(lo, SPAN - QROWS)
            rows = pl.ds(pl.multiple_of(at, 16), QROWS)
            row = iota((QROWS, DIM), 0) + at
            live = (row >= jnp.maximum(off, lo)) & (row < jnp.minimum(off + n, lo + QROWS))

            for size in range(1, 9):
                @pl.when(count == size)
                def _():
                    query = qs[rows, :]
                    spans = [pl.ds(pl.multiple_of(list_ref[c, j] * CLUSTER, CLUSTER), CLUSTER)
                             for j in range(size)]
                    scores = [dot_nt(query, kc[spans[j], :]) for j in range(size)]
                    top = functools.reduce(jnp.maximum, scores)
                    top = jnp.max(top, axis=1, keepdims=True)
                    powers = [jnp.exp2((s - top) * factor) for s in scores]
                    total = jnp.sum(functools.reduce(jnp.add, powers), axis=1, keepdims=True)
                    mixed = functools.reduce(jnp.add, [
                        jnp.dot(powers[j].astype(bf16), vc[spans[j], :], preferred_element_type=f32)
                        for j in range(size)])
                    acc[rows, :] = jnp.where(live, mixed / total, acc[rows, :])
            return 0

        lax.fori_loop(0, windows, window, 0)
        return 0

    lax.fori_loop(0, CLUSTERS, attend, 0)

    def finish(i, _):
        rows = pl.ds(pl.multiple_of(i * 512, 512), 512)
        out[rows, :] = acc[rows, :].astype(bf16)
        return 0

    lax.fori_loop(0, SPAN // 512, finish, 0)


def attend_call(off, cnt, listed, ext, rep, kall, vall, qs):
    smem = pl.BlockSpec(memory_space=pltpu.SMEM)
    vmem = pl.BlockSpec(memory_space=pltpu.VMEM)
    return pl.pallas_call(
        attend_kernel,
        out_shape=jax.ShapeDtypeStruct((SPAN, DIM), bf16),
        in_specs=[smem] * 5 + [vmem] * 3,
        out_specs=vmem,
        scratch_shapes=[
            pltpu.VMEM((TOKENS, DIM), bf16),
            pltpu.VMEM((TOKENS, DIM), bf16),
            pltpu.VMEM((SPAN, DIM), f32),
        ],
        compiler_params=pltpu.CompilerParams(vmem_limit_bytes=48 * 2**20),
        name="attend",
    )(off, cnt, listed, ext, rep, kall, vall, qs)


HALF = HEADS // 2


def return_kernel(mixed, destt_ref, out, partner_s, both_s, onehot, tx, swap_send, swap_recv,
                  send_sem, recv_sem, own_sem):
    guide, me = lax.axis_index("guide"), lax.axis_index("seq")
    other = 1 - guide
    head_guide, head_col = me // HALF, me % HALF

    barrier = pltpu.get_barrier_semaphore()
    pl.semaphore_signal(barrier, inc=1, device_id={"guide": other}, device_id_type=MESH)

    def greet(step, _):
        i = lax.rem(head_col + step, HALF)
        pl.semaphore_signal(barrier, inc=1, device_id={"guide": head_guide, "seq": guide * HALF + i},
                            device_id_type=MESH)
        return 0

    lax.fori_loop(1, HALF, greet, 0)

    @pl.when(head_guide != guide)
    def _():
        greet(0, 0)
        pl.semaphore_wait(barrier, HALF + 1)

    @pl.when(head_guide == guide)
    def _():
        pl.semaphore_wait(barrier, HALF)

    swap = pltpu.make_async_remote_copy(
        src_ref=mixed, dst_ref=partner_s, send_sem=swap_send, recv_sem=swap_recv,
        device_id={"guide": other}, device_id_type=MESH)
    swap.start()

    destt = destt_ref[...]
    picked = jnp.where(guide == 0, destt[:, :HALF], destt[:, HALF:])
    for i in range(HALF):
        for c in range(SPAN // 512):
            onehot[i * LOCAL:(i + 1) * LOCAL, c * 512:(c + 1) * 512] = jnp.where(
                picked[:, i:i + 1] == iota((LOCAL, 512), 1) + c * 512, 1.0, 0.0).astype(bf16)
    swap.wait()

    def combine(c, _):
        rows = pl.ds(pl.multiple_of(c * 512, 512), 512)
        own = mixed[rows, :].astype(f32)
        far = partner_s[rows, :].astype(f32)
        conditioned = jnp.where(guide == 0, own, far)
        unconditioned = jnp.where(guide == 0, far, own)
        both_s[rows, :] = (unconditioned + GUIDE_SCALE * (conditioned - unconditioned)).astype(bf16)
        return 0

    lax.fori_loop(0, SPAN // 512, combine, 0)

    def place(col):
        return out.at[:, pl.ds(pl.multiple_of(col * DIM, DIM), DIM)]

    def send_copy(i):
        return pltpu.make_async_remote_copy(
            src_ref=tx.at[i], dst_ref=place(head_col), send_sem=send_sem.at[i],
            recv_sem=recv_sem.at[head_col],
            device_id={"guide": head_guide, "seq": guide * HALF + i}, device_id_type=MESH)

    def wait_copy(col):
        return pltpu.make_async_remote_copy(
            src_ref=tx.at[col], dst_ref=place(col), send_sem=send_sem.at[col],
            recv_sem=recv_sem.at[col], device_id={"guide": other}, device_id_type=MESH)

    own_copy = pltpu.make_async_copy(tx.at[head_col], place(head_col), own_sem)

    def restore(i):
        rows = pl.ds(pl.multiple_of(i * LOCAL, LOCAL), LOCAL)
        tx[i] = jnp.dot(onehot[rows, :], both_s[...], preferred_element_type=f32).astype(bf16)

    def step(j, _):
        i = lax.rem(head_col + j, HALF)
        restore(i)
        send_copy(i).start()
        return 0

    lax.fori_loop(1, HALF, step, 0)
    restore(head_col)

    @pl.when(head_guide == guide)
    def _():
        own_copy.start()

    @pl.when(head_guide != guide)
    def _():
        send_copy(head_col).start()

    def finish(j, _):
        i = lax.rem(head_col + j, HALF)
        send_copy(i).wait_send()
        wait_copy(i).wait_recv()
        return 0

    lax.fori_loop(1, HALF, finish, 0)

    @pl.when(head_guide == guide)
    def _():
        own_copy.wait()

    @pl.when(head_guide != guide)
    def _():
        send_copy(head_col).wait_send()
        wait_copy(head_col).wait_recv()


def return_call(mixed, destt):
    vmem = pl.BlockSpec(memory_space=pltpu.VMEM)
    return pl.pallas_call(
        return_kernel,
        out_shape=jax.ShapeDtypeStruct((LOCAL, HALF * DIM), bf16),
        in_specs=[vmem, vmem],
        out_specs=pl.BlockSpec(memory_space=pl.ANY),
        scratch_shapes=[
            pltpu.VMEM((SPAN, DIM), bf16),
            pltpu.VMEM((SPAN, DIM), bf16),
            pltpu.VMEM((SPAN // 2, SPAN), bf16),
            pltpu.VMEM((HALF, LOCAL, DIM), bf16),
            pltpu.SemaphoreType.DMA,
            pltpu.SemaphoreType.DMA,
            pltpu.SemaphoreType.DMA((HALF,)),
            pltpu.SemaphoreType.DMA((HALF,)),
            pltpu.SemaphoreType.DMA,
        ],
        compiler_params=pltpu.CompilerParams(
            collective_id=1, has_side_effects=True, vmem_limit_bytes=48 * 2**20),
        name="return_tokens",
    )(mixed, destt)


def on_device(queries, key_vectors, value_vectors, cluster_order, key_blocks, extents):
    order = cluster_order.reshape(128, 128)
    kall, vall, qs, dest, destt = gather_call(
        queries[0], key_vectors[0], value_vectors[0], order)
    rep_of = (cluster_order.reshape(CLUSTERS, CLUSTER) // LOCAL) % REPS
    cnt = jnp.stack([jnp.sum((rep_of == r).astype(i32), axis=1) for r in range(REPS)])
    off = jnp.cumsum(cnt, axis=1) - cnt
    rep = lax.axis_index("rep").astype(i32).reshape(1)
    mixed = attend_call(off, cnt, key_blocks[0], extents[0], rep, kall, vall, qs)
    return return_call(mixed, destt)


def solution(mesh):
    placed = (
        P("guide", ("seq", "rep"), None),
        P("guide", ("seq", "rep"), None),
        P("guide", ("seq", "rep"), None),
        P("seq", None),
        P("seq", None, None),
        P("seq", None),
    )
    return jax.shard_map(
        on_device, mesh=mesh, in_specs=placed, out_specs=P(("seq", "rep"), "guide"), check_vma=False
    )
```

```python
import functools

import jax
import jax.numpy as jnp
from jax import lax
from jax.experimental import pallas as pl
from jax.experimental.pallas import tpu as pltpu
from jax.sharding import PartitionSpec as P

MESH = pl.DeviceIdType.MESH
CLUSTER = 256
GUIDE_SCALE = 5.0
HEADS = 32
SEQ_X, SEQ_Z = 4, 8
REPS = 4
TOKENS = 16384
DIM = 128
SPAN = TOKENS // REPS
LOCAL = 128
CLUSTERS = TOKENS // CLUSTER
CHUNK = 512
CHUNKS = SPAN // CHUNK
WINDOW = 128
QROWS = 96
f32, bf16, i32 = jnp.float32, jnp.bfloat16, jnp.int32

NT = (((1,), (1,)), ((), ()))


def dot_nt(a, b):
    return lax.dot_general(a, b, NT, preferred_element_type=f32)


def iota(shape, dim):
    return lax.broadcasted_iota(i32, shape, dim)


def gather_kernel(q_in, k_in, v_in, order_ref, kall, vall, qs, dest_out, destt_out,
                  rx, sorted_, onehot, key_s, low_s, rhi_s, rlo_s, dest_s, destt_s,
                  send_sem, recv_sem, own_sem, ysend, yrecv, out_sem):
    me = lax.axis_index("seq")
    rep = lax.axis_index("rep")
    x, z = me // SEQ_Z, me % SEQ_Z
    right, left = lax.rem(rep + 1, REPS), lax.rem(rep + REPS - 1, REPS)
    ins = (k_in, v_in, q_in)
    alls = (kall, vall)

    def peer_of(off):
        return lax.rem(x + off // SEQ_Z, SEQ_X) * SEQ_Z + lax.rem(z + off % SEQ_Z, SEQ_Z)

    barrier = pltpu.get_barrier_semaphore()

    def greet(off, _):
        pl.semaphore_signal(barrier, inc=1, device_id={"seq": peer_of(off)}, device_id_type=MESH)
        return 0

    lax.fori_loop(1, HEADS, greet, 0)
    pl.semaphore_signal(barrier, inc=1, device_id={"rep": right}, device_id_type=MESH)
    pl.semaphore_signal(barrier, inc=1, device_id={"rep": left}, device_id_type=MESH)
    pl.semaphore_wait(barrier, HEADS - 1 + 2)

    def a2a_copy(a, peer, slot):
        return pltpu.make_async_remote_copy(
            src_ref=ins[a].at[:, pl.ds(pl.multiple_of(peer * DIM, DIM), DIM)],
            dst_ref=rx.at[a, slot],
            send_sem=send_sem.at[a, peer], recv_sem=recv_sem.at[a, slot],
            device_id={"seq": peer}, device_id_type=MESH)

    def own_copy(a):
        return pltpu.make_async_copy(
            ins[a].at[:, pl.ds(pl.multiple_of(me * DIM, DIM), DIM)], rx.at[a, me], own_sem.at[a])

    for a in range(3):
        own_copy(a).start()

        def send(off, _):
            a2a_copy(a, peer_of(off), me).start()
            return 0

        lax.fori_loop(1, HEADS, send, 0)

    order = order_ref[...]
    block = order >> 7
    mine = (block & (REPS - 1)) == rep
    key_s[...] = jnp.where(mine, block >> 2, -1)
    low_s[...] = order & (LOCAL - 1)
    present = jnp.where(mine, 1.0, 0.0).astype(bf16)
    rows, cols = iota((128, 128), 0), iota((128, 128), 1)
    upper = jnp.where(rows < cols, 1.0, 0.0).astype(bf16)
    lower = jnp.where(cols < rows, 1.0, 0.0).astype(bf16)
    ones = jnp.ones((128, 128), bf16)
    within = jnp.dot(present, upper, preferred_element_type=f32)
    totals = jnp.dot(present, ones, preferred_element_type=f32).astype(bf16)
    rank = within + jnp.dot(lower, totals, preferred_element_type=f32)
    rank_hi = jnp.floor(rank * (1.0 / 64.0))
    rhi_s[...] = rank_hi
    rlo_s[...] = rank - 64.0 * rank_hi

    def accumulate(step, carry):
        d, dt = carry
        his, los, bs = [], [], []
        base = pl.multiple_of(step * 8, 8)
        key8, low8 = key_s[pl.ds(base, 8), :], low_s[pl.ds(base, 8), :]
        rhi8, rlo8 = rhi_s[pl.ds(base, 8), :], rlo_s[pl.ds(base, 8), :]
        for j in range(8):
            hit = iota((HEADS, 128), 0) == key8[j:j + 1]
            his.append(jnp.where(hit, rhi8[j:j + 1], 0.0))
            los.append(jnp.where(hit, rlo8[j:j + 1], 0.0))
            bs.append(jnp.where(iota((128, 128), 0) == low8[j:j + 1], 1.0, 0.0))
        left_m = jnp.concatenate([jnp.concatenate(his, 1), jnp.concatenate(los, 1)], 0).astype(bf16)
        right_m = jnp.concatenate(bs, 1).astype(bf16)
        return d + dot_nt(left_m, right_m), dt + dot_nt(right_m, left_m)

    d, dt = lax.fori_loop(0, 16, accumulate, (jnp.zeros((2 * HEADS, 128), f32), jnp.zeros((128, 2 * HEADS), f32)))
    dest_s[...] = (64.0 * d[:HEADS] + d[HEADS:]).astype(i32)
    destt_s[...] = (64.0 * dt[:, :HEADS] + dt[:, HEADS:]).astype(i32)
    dest_copy = pltpu.make_async_copy(dest_s, dest_out, out_sem.at[0])
    destt_copy = pltpu.make_async_copy(destt_s, destt_out, out_sem.at[1])
    dest_copy.start()
    destt_copy.start()

    def build(kb, _):
        base = pl.multiple_of(kb * 256, 256)
        row = iota((256, 128), 0) + base
        for s in range(HEADS):
            onehot[pl.ds(base, 256), s * 128:(s + 1) * 128] = jnp.where(
                row == dest_s[s:s + 1, :], 1.0, 0.0).astype(bf16)
        return 0

    lax.fori_loop(0, SPAN // 256, build, 0)

    def wait_in(a):
        def one(off, _):
            a2a_copy(a, me, peer_of(off)).wait_recv()
            return 0

        lax.fori_loop(1, HEADS, one, 0)
        own_copy(a).wait()

    def rows_of(c):
        return pl.ds(pl.multiple_of(c * CHUNK, CHUNK), CHUNK)

    def ycopy(a, kind, c):
        if kind == 0:
            src, slot, to = sorted_.at[a, rows_of(c)], rep, right
        elif kind == 1:
            src, slot, to = sorted_.at[a, rows_of(c)], rep, left
        else:
            even = lax.rem(c, 2) == 0
            slot = jnp.where(even, left, right)
            to = jnp.where(even, right, left)
            src = alls[a].at[slot, rows_of(c)]
        return pltpu.make_async_remote_copy(
            src_ref=src, dst_ref=alls[a].at[slot, rows_of(c)],
            send_sem=ysend.at[a, kind, c], recv_sem=yrecv.at[a, kind, c],
            device_id={"rep": to}, device_id_type=MESH)

    def keep_copy(a, c):
        to = alls[a].at[rep, rows_of(c)] if a < 2 else qs.at[rows_of(c)]
        return pltpu.make_async_copy(sorted_.at[a, rows_of(c)], to, out_sem.at[2 + a * CHUNKS + c])

    def wait_y(a, kind, c):
        if kind == 0:
            slot = left
        elif kind == 1:
            slot = right
        else:
            slot = lax.rem(rep + 2, REPS)
        pltpu.make_async_remote_copy(
            src_ref=sorted_.at[a, rows_of(c)], dst_ref=alls[a].at[slot, rows_of(c)],
            send_sem=ysend.at[a, kind, c], recv_sem=yrecv.at[a, kind, c],
            device_id={"rep": right}, device_id_type=MESH).wait_recv()

    def forward(a, c):
        wait_y(a, 0, c)
        wait_y(a, 1, c)
        ycopy(a, 2, c).start()

    for a in range(3):
        wait_in(a)

        def sort(c, _):
            sorted_[a, rows_of(c)] = jnp.dot(
                onehot[rows_of(c), :], rx[a].reshape(SPAN, DIM), preferred_element_type=f32).astype(bf16)
            if a < 2:
                ycopy(a, 0, c).start()
                ycopy(a, 1, c).start()
            keep_copy(a, c).start()
            if a > 0:
                forward(a - 1, c)
            return 0

        lax.fori_loop(0, CHUNKS, sort, 0)

    dest_copy.wait()
    destt_copy.wait()

    def finish(c, _):
        for a in range(3):
            keep_copy(a, c).wait()
        for a in range(2):
            wait_y(a, 2, c)
            for kind in range(3):
                ycopy(a, kind, c).wait_send()
        return 0

    lax.fori_loop(0, CHUNKS, finish, 0)

    def sent(off, _):
        for a in range(3):
            a2a_copy(a, peer_of(off), me).wait_send()
        return 0

    lax.fori_loop(1, HEADS, sent, 0)


def gather_call(q, k, v, order):
    any_ = pl.BlockSpec(memory_space=pl.ANY)
    vmem = pl.BlockSpec(memory_space=pltpu.VMEM)
    return pl.pallas_call(
        gather_kernel,
        out_shape=(
            jax.ShapeDtypeStruct((REPS, SPAN, DIM), bf16),
            jax.ShapeDtypeStruct((REPS, SPAN, DIM), bf16),
            jax.ShapeDtypeStruct((SPAN, DIM), bf16),
            jax.ShapeDtypeStruct((HEADS, LOCAL), i32),
            jax.ShapeDtypeStruct((LOCAL, HEADS), i32),
        ),
        in_specs=[any_, any_, any_, vmem],
        out_specs=(any_,) * 5,
        scratch_shapes=[
            pltpu.VMEM((3, HEADS, LOCAL, DIM), bf16),
            pltpu.VMEM((3, SPAN, DIM), bf16),
            pltpu.VMEM((SPAN, SPAN), bf16),
            pltpu.VMEM((128, 128), i32),
            pltpu.VMEM((128, 128), i32),
            pltpu.VMEM((128, 128), f32),
            pltpu.VMEM((128, 128), f32),
            pltpu.VMEM((HEADS, LOCAL), i32),
            pltpu.VMEM((LOCAL, HEADS), i32),
            pltpu.SemaphoreType.DMA((3, HEADS)),
            pltpu.SemaphoreType.DMA((3, HEADS)),
            pltpu.SemaphoreType.DMA((3,)),
            pltpu.SemaphoreType.DMA((2, 3, CHUNKS)),
            pltpu.SemaphoreType.DMA((2, 3, CHUNKS)),
            pltpu.SemaphoreType.DMA((2 + 3 * CHUNKS,)),
        ],
        compiler_params=pltpu.CompilerParams(
            collective_id=0, has_side_effects=True, vmem_limit_bytes=56 * 2**20),
        name="gather_sorted",
    )(q, k, v, order)


GROUP = 4


def attend_kernel(off_ref, cnt_ref, list_ref, ext_ref, perm_ref, rep_ref, kall, vall, qs, out, kc, vc, acc):
    ones = jnp.ones((CLUSTER, DIM), bf16)

    def span(c):
        return pl.ds(pl.multiple_of(c * CLUSTER, CLUSTER), CLUSTER)

    def compact_slow(c):
        def window(k, whole):
            start = jnp.int32(0)
            for r in range(REPS):
                off, n = off_ref[r, c], cnt_ref[r, c]
                lo = (off // 16) * 16 + k * WINDOW
                at = pl.multiple_of(jnp.minimum(lo, SPAN - WINDOW), 16)
                first, last = jnp.maximum(off, lo), jnp.minimum(off + n, lo + WINDOW)
                shift = start - off
                m = iota((CLUSTER, WINDOW), 0)
                hit = (m - iota((CLUSTER, WINDOW), 1) == at + shift) & (m >= first + shift) & (m < last + shift)
                kv = jnp.concatenate([kall[r, pl.ds(at, WINDOW), :], vall[r, pl.ds(at, WINDOW), :]], 1)
                whole = whole + jnp.dot(jnp.where(hit, 1.0, 0.0).astype(bf16), kv, preferred_element_type=f32)
                start = start + n
            return whole

        whole = lax.fori_loop(0, 3, window, jnp.zeros((CLUSTER, 2 * DIM), f32))
        kc[span(c), :] = whole[:, :DIM].astype(bf16)
        vc[span(c), :DIM] = whole[:, DIM:].astype(bf16)

    def compact_fast(c):
        m = iota((CLUSTER, WINDOW), 0)
        start, target = jnp.int32(0), None
        keys, vals = [], []
        for r in range(REPS):
            off = off_ref[r, c]
            at = pl.multiple_of(jnp.minimum((off // 16) * 16, SPAN - WINDOW), 16)
            moved = m + (off - at - start + r * WINDOW)
            target = moved if r == 0 else jnp.where(m >= start, moved, target)
            keys.append(kall[r, pl.ds(at, WINDOW), :])
            vals.append(vall[r, pl.ds(at, WINDOW), :])
            start = start + cnt_ref[r, c]
        lane = iota((CLUSTER, WINDOW), 1)
        hot = jnp.concatenate(
            [jnp.where(target == lane + r * WINDOW, 1.0, 0.0).astype(bf16) for r in range(REPS)], 1)
        kv = jnp.concatenate([jnp.concatenate(keys, 0), jnp.concatenate(vals, 0)], 1)
        whole = jnp.dot(hot, kv, preferred_element_type=f32)
        kc[span(c), :] = whole[:, :DIM].astype(bf16)
        vc[span(c), :] = jnp.concatenate([whole[:, DIM:].astype(bf16), ones], 1)

    def long_pieces(c):
        most = jnp.int32(0)
        for r in range(REPS):
            most = jnp.maximum(most, off_ref[r, c] % 16 + cnt_ref[r, c])
        return most > WINDOW

    def compact(i, _):
        cs = [i * GROUP + u for u in range(GROUP)]
        for c in cs:
            compact_fast(c)
        for c in cs:
            @pl.when(long_pieces(c))
            def _():
                compact_slow(c)
        return 0

    lax.fori_loop(0, CLUSTERS // GROUP, compact, 0)

    rep = rep_ref[0]
    factor = DIM ** -0.5 * 1.4426950408889634

    def attend_rows(cs, k, size):
        rows, live, blocks, tops, scores = [], [], [], [], []
        for c in cs:
            off, n = off_ref[rep, c], cnt_ref[rep, c]
            lo = (off // 16) * 16 + k * QROWS
            at = jnp.minimum(lo, SPAN - QROWS)
            rows.append(pl.ds(pl.multiple_of(at, 16), QROWS))
            row = iota((QROWS, DIM), 0) + at
            live.append((row >= jnp.maximum(off, lo)) & (row < jnp.minimum(off + n, lo + QROWS)))
            blocks.append([span(list_ref[c, jnp.where(j < ext_ref[c], j, 0)]) for j in range(size)])
        for u in range(len(cs)):
            query = qs[rows[u], :]
            scores.append([dot_nt(query, kc[b, :]) for b in blocks[u]])
        for u in range(len(cs)):
            tops.append(jnp.max(functools.reduce(jnp.maximum, scores[u]), axis=1, keepdims=True))
        results = []
        for u, c in enumerate(cs):
            mixed = None
            for j in range(size):
                top = tops[u] if j == 0 else jnp.where(j < ext_ref[c], tops[u], jnp.inf)
                power = jnp.exp2((scores[u][j] - top) * factor).astype(bf16)
                part = jnp.dot(power, vc[blocks[u][j], :], preferred_element_type=f32)
                mixed = part if mixed is None else mixed + part
            results.append(mixed[:, :DIM] / mixed[:, DIM:])
        for u in range(len(cs)):
            acc[rows[u], :] = jnp.where(live[u], results[u], acc[rows[u], :])

    def attend(g, _):
        cs = [perm_ref[g * GROUP + u] for u in range(GROUP)]
        size_most = ext_ref[cs[-1]]
        for size in range(1, 9):
            @pl.when(size_most == size)
            def _():
                attend_rows(cs, 0, size)
        for c in cs:
            off, n = off_ref[rep, c], cnt_ref[rep, c]

            def more(k, _):
                attend_rows([c], k, 8)
                return 0

            lax.fori_loop(1, (off % 16 + n + QROWS - 1) // QROWS, more, 0)
        return 0

    lax.fori_loop(0, CLUSTERS // GROUP, attend, 0)

    def finish(i, _):
        rows = pl.ds(pl.multiple_of(i * 512, 512), 512)
        out[rows, :] = acc[rows, :].astype(bf16)
        return 0

    lax.fori_loop(0, SPAN // 512, finish, 0)


def attend_call(off, cnt, listed, ext, perm, rep, kall, vall, qs):
    smem = pl.BlockSpec(memory_space=pltpu.SMEM)
    vmem = pl.BlockSpec(memory_space=pltpu.VMEM)
    return pl.pallas_call(
        attend_kernel,
        out_shape=jax.ShapeDtypeStruct((SPAN, DIM), bf16),
        in_specs=[smem] * 6 + [vmem] * 3,
        out_specs=vmem,
        scratch_shapes=[
            pltpu.VMEM((TOKENS, DIM), bf16),
            pltpu.VMEM((TOKENS, 2 * DIM), bf16),
            pltpu.VMEM((SPAN, DIM), f32),
        ],
        compiler_params=pltpu.CompilerParams(vmem_limit_bytes=56 * 2**20),
        name="attend",
    )(off, cnt, listed, ext, perm, rep, kall, vall, qs)


HALF = HEADS // 2


def return_kernel(mixed, destt_ref, out, partner_s, both_s, onehot, tx, swap_send, swap_recv,
                  send_sem, recv_sem, own_sem):
    guide, me = lax.axis_index("guide"), lax.axis_index("seq")
    other = 1 - guide
    head_guide, head_col = me // HALF, me % HALF

    barrier = pltpu.get_barrier_semaphore()
    pl.semaphore_signal(barrier, inc=1, device_id={"guide": other}, device_id_type=MESH)

    def greet(step, _):
        i = lax.rem(head_col + step, HALF)
        pl.semaphore_signal(barrier, inc=1, device_id={"guide": head_guide, "seq": guide * HALF + i},
                            device_id_type=MESH)
        return 0

    lax.fori_loop(1, HALF, greet, 0)

    @pl.when(head_guide != guide)
    def _():
        greet(0, 0)
        pl.semaphore_wait(barrier, HALF + 1)

    @pl.when(head_guide == guide)
    def _():
        pl.semaphore_wait(barrier, HALF)

    swap = pltpu.make_async_remote_copy(
        src_ref=mixed, dst_ref=partner_s, send_sem=swap_send, recv_sem=swap_recv,
        device_id={"guide": other}, device_id_type=MESH)
    swap.start()

    destt = destt_ref[...]
    picked = jnp.where(guide == 0, destt[:, :HALF], destt[:, HALF:])
    for i in range(HALF):
        for c in range(SPAN // 512):
            onehot[i * LOCAL:(i + 1) * LOCAL, c * 512:(c + 1) * 512] = jnp.where(
                picked[:, i:i + 1] == iota((LOCAL, 512), 1) + c * 512, 1.0, 0.0).astype(bf16)
    swap.wait()

    def combine(c, _):
        rows = pl.ds(pl.multiple_of(c * 512, 512), 512)
        own = mixed[rows, :].astype(f32)
        far = partner_s[rows, :].astype(f32)
        conditioned = jnp.where(guide == 0, own, far)
        unconditioned = jnp.where(guide == 0, far, own)
        both_s[rows, :] = (unconditioned + GUIDE_SCALE * (conditioned - unconditioned)).astype(bf16)
        return 0

    lax.fori_loop(0, SPAN // 512, combine, 0)

    def place(col):
        return out.at[:, pl.ds(pl.multiple_of(col * DIM, DIM), DIM)]

    def send_copy(i):
        return pltpu.make_async_remote_copy(
            src_ref=tx.at[i], dst_ref=place(head_col), send_sem=send_sem.at[i],
            recv_sem=recv_sem.at[head_col],
            device_id={"guide": head_guide, "seq": guide * HALF + i}, device_id_type=MESH)

    def wait_copy(col):
        return pltpu.make_async_remote_copy(
            src_ref=tx.at[col], dst_ref=place(col), send_sem=send_sem.at[col],
            recv_sem=recv_sem.at[col], device_id={"guide": other}, device_id_type=MESH)

    own_copy = pltpu.make_async_copy(tx.at[head_col], place(head_col), own_sem)

    def restore(i):
        rows = pl.ds(pl.multiple_of(i * LOCAL, LOCAL), LOCAL)
        tx[i] = jnp.dot(onehot[rows, :], both_s[...], preferred_element_type=f32).astype(bf16)

    def step(j, _):
        i = lax.rem(head_col + j, HALF)
        restore(i)
        send_copy(i).start()
        return 0

    lax.fori_loop(1, HALF, step, 0)
    restore(head_col)

    @pl.when(head_guide == guide)
    def _():
        own_copy.start()

    @pl.when(head_guide != guide)
    def _():
        send_copy(head_col).start()

    def finish(j, _):
        i = lax.rem(head_col + j, HALF)
        send_copy(i).wait_send()
        wait_copy(i).wait_recv()
        return 0

    lax.fori_loop(1, HALF, finish, 0)

    @pl.when(head_guide == guide)
    def _():
        own_copy.wait()

    @pl.when(head_guide != guide)
    def _():
        send_copy(head_col).wait_send()
        wait_copy(head_col).wait_recv()


def return_call(mixed, destt):
    vmem = pl.BlockSpec(memory_space=pltpu.VMEM)
    return pl.pallas_call(
        return_kernel,
        out_shape=jax.ShapeDtypeStruct((LOCAL, HALF * DIM), bf16),
        in_specs=[vmem, vmem],
        out_specs=pl.BlockSpec(memory_space=pl.ANY),
        scratch_shapes=[
            pltpu.VMEM((SPAN, DIM), bf16),
            pltpu.VMEM((SPAN, DIM), bf16),
            pltpu.VMEM((SPAN // 2, SPAN), bf16),
            pltpu.VMEM((HALF, LOCAL, DIM), bf16),
            pltpu.SemaphoreType.DMA,
            pltpu.SemaphoreType.DMA,
            pltpu.SemaphoreType.DMA((HALF,)),
            pltpu.SemaphoreType.DMA((HALF,)),
            pltpu.SemaphoreType.DMA,
        ],
        compiler_params=pltpu.CompilerParams(
            collective_id=1, has_side_effects=True, vmem_limit_bytes=48 * 2**20),
        name="return_tokens",
    )(mixed, destt)


def on_device(queries, key_vectors, value_vectors, cluster_order, key_blocks, extents):
    order = cluster_order.reshape(128, 128)
    kall, vall, qs, dest, destt = gather_call(
        queries[0], key_vectors[0], value_vectors[0], order)
    rep_of = (cluster_order.reshape(CLUSTERS, CLUSTER) // LOCAL) % REPS
    cnt = jnp.stack([jnp.sum((rep_of == r).astype(i32), axis=1) for r in range(REPS)])
    off = jnp.cumsum(cnt, axis=1) - cnt
    rep = lax.axis_index("rep").astype(i32).reshape(1)
    ext = extents[0]
    index = jnp.arange(CLUSTERS, dtype=i32)
    before = (ext[None, :] < ext[:, None]) | ((ext[None, :] == ext[:, None]) & (index[None, :] < index[:, None]))
    place = jnp.sum(before.astype(i32), axis=1)
    perm = jnp.sum(jnp.where(place[None, :] == index[:, None], index[None, :], 0), axis=1)
    mixed = attend_call(off, cnt, key_blocks[0], ext, perm, rep, kall, vall, qs)
    return return_call(mixed, destt)


def solution(mesh):
    placed = (
        P("guide", ("seq", "rep"), None),
        P("guide", ("seq", "rep"), None),
        P("guide", ("seq", "rep"), None),
        P("seq", None),
        P("seq", None, None),
        P("seq", None),
    )
    return jax.shard_map(
        on_device, mesh=mesh, in_specs=placed, out_specs=P(("seq", "rep"), "guide"), check_vma=False
    )
```

```python
import functools

import jax
import jax.numpy as jnp
from jax import lax
from jax.experimental import pallas as pl
from jax.experimental.pallas import tpu as pltpu
from jax.sharding import PartitionSpec as P

MESH = pl.DeviceIdType.MESH
CLUSTER = 256
GUIDE_SCALE = 5.0
HEADS = 32
SEQ_X, SEQ_Z = 4, 8
REPS = 4
TOKENS = 16384
DIM = 128
SPAN = TOKENS // REPS
LOCAL = 128
CLUSTERS = TOKENS // CLUSTER
CHUNK = 512
CHUNKS = SPAN // CHUNK
GROUPS = 2
SLOTS = HEADS // GROUPS
LIST = SPAN // GROUPS
WINDOW = 64
QROWS = 96
f32, bf16, i32 = jnp.float32, jnp.bfloat16, jnp.int32

NT = (((1,), (1,)), ((), ()))


def dot_nt(a, b):
    return lax.dot_general(a, b, NT, preferred_element_type=f32)


def iota(shape, dim):
    return lax.broadcasted_iota(i32, shape, dim)


def z_distance(group, i):
    return i + (i // 2) * 2 + (i // 3) * 2 if group == 0 else i + 2 + i // 2


def gather_kernel(q_in, k_in, v_in, order_in, ext_ref, kall, vall, qs, table_out, destt_out,
                  rx, sorted_, onehot, order_s, key_s, low_s, rank_s, dest_s, destt_s, table_s,
                  send_sem, recv_sem, own_sem, order_sem, ysend, yrecv, keep_sem, out_sem):
    me = lax.axis_index("seq")
    rep = lax.axis_index("rep")
    x, z = me // SEQ_Z, me % SEQ_Z
    right, left = lax.rem(rep + 1, REPS), lax.rem(rep + REPS - 1, REPS)
    ins = (k_in, v_in, q_in)
    alls = (kall, vall)

    def at_distance(group, slot, sign):
        dx, dz = slot // 4, z_distance(group, slot % 4)
        return lax.rem(x + sign * dx + SEQ_X, SEQ_X) * SEQ_Z + lax.rem(z + sign * dz + SEQ_Z, SEQ_Z)

    def order_copy(u):
        return pltpu.make_async_copy(
            order_in.at[:, pl.ds(pl.multiple_of(u * 128, 128), 128)], order_s.at[pl.ds(u, 1), :], order_sem.at[u])

    def fetch(u, _):
        order_copy(u).start()
        return 0

    lax.fori_loop(0, 128, fetch, 0)

    barrier = pltpu.get_barrier_semaphore()
    for group in range(GROUPS):
        def greet(slot, _):
            pl.semaphore_signal(barrier, inc=1, device_id={"seq": at_distance(group, slot, 1)}, device_id_type=MESH)
            return 0

        lax.fori_loop(1 - group, SLOTS, greet, 0)
    pl.semaphore_signal(barrier, inc=1, device_id={"rep": right}, device_id_type=MESH)
    pl.semaphore_signal(barrier, inc=1, device_id={"rep": left}, device_id_type=MESH)
    pl.semaphore_wait(barrier, HEADS - 1 + 2)

    def a2a_copy(a, group, slot):
        peer = at_distance(group, slot, 1)
        return pltpu.make_async_remote_copy(
            src_ref=ins[a].at[:, pl.ds(pl.multiple_of(peer * DIM, DIM), DIM)],
            dst_ref=rx.at[a, group, pl.ds(pl.multiple_of(slot * LOCAL, LOCAL), LOCAL)],
            send_sem=send_sem.at[a, group, slot], recv_sem=recv_sem.at[a, group, slot],
            device_id={"seq": peer}, device_id_type=MESH)

    def own_copy(a):
        return pltpu.make_async_copy(
            ins[a].at[:, pl.ds(pl.multiple_of(me * DIM, DIM), DIM)], rx.at[a, 0, pl.ds(0, LOCAL)], own_sem.at[a])

    for a in range(3):
        own_copy(a).start()
        for group in range(GROUPS):
            def send(slot, _):
                a2a_copy(a, group, slot).start()
                return 0

            lax.fori_loop(1 - group, SLOTS, send, 0)

    def fetched(u, _):
        order_copy(u).wait()
        return 0

    lax.fori_loop(0, 128, fetched, 0)

    order = order_s[...]
    block = order >> 7
    owner = block & (REPS - 1)
    away = (z - (block >> 2)) & (SEQ_Z - 1)
    second = jnp.where((away == 0) | (away == 1) | (away == 4) | (away == 7), 0, 1)
    mine = owner == rep
    rows, cols = iota((128, 128), 0), iota((128, 128), 1)
    as_mask = lambda hit: jnp.where(hit, 1.0, 0.0).astype(bf16)
    product = lambda a, b: jnp.dot(a, b, preferred_element_type=f32)
    upper, lower = as_mask(rows < cols), as_mask(cols < rows)
    to_cluster, past_cluster = as_mask(cols < (rows >> 1) * 2), as_mask(cols < (rows >> 1) * 2 + 2)
    ones = jnp.ones((128, 128), bf16)
    ranks, befores, pasts = [], [], []
    for group in range(GROUPS):
        present = as_mask(mine & (second == group))
        totals = product(present, ones).astype(bf16)
        ranks.append(product(present, upper) + product(lower, totals))
        befores.append(product(to_cluster, totals))
        pasts.append(product(past_cluster, totals))
    rank = jnp.where(second == 0, ranks[0], ranks[1])
    whole = jnp.where(second == 0, ranks[0] + befores[1], ranks[1] + pasts[0])
    rank_hi, whole_hi = jnp.floor(rank * (1.0 / 64.0)), jnp.floor(whole * (1.0 / 64.0))
    key_s[...] = jnp.where(mine, block >> 2, -1)
    low_s[...] = order & (LOCAL - 1)
    rank_s[0] = rank_hi
    rank_s[1] = rank - 64.0 * rank_hi
    rank_s[2] = whole_hi
    rank_s[3] = whole - 64.0 * whole_hi

    def accumulate(step, carry):
        d, dt = carry
        parts, bs = [[], [], [], []], []
        base = pl.multiple_of(step * 32, 32)
        key8, low8 = key_s[pl.ds(base, 32), :], low_s[pl.ds(base, 32), :]
        rank8 = [rank_s[i, pl.ds(base, 32), :] for i in range(4)]
        for j in range(32):
            hit = iota((HEADS, 128), 0) == key8[j:j + 1]
            for i in range(4):
                parts[i].append(jnp.where(hit, rank8[i][j:j + 1], 0.0).astype(bf16))
            bs.append(as_mask(iota((128, 128), 0) == low8[j:j + 1]))
        parts = [jnp.concatenate(p, 1) for p in parts]
        right_m = jnp.concatenate(bs, 1)
        d = d + dot_nt(jnp.concatenate(parts[:2], 0), right_m)
        dt = dt + dot_nt(right_m, jnp.concatenate(parts[2:], 0))
        return d, dt

    d, dt = lax.fori_loop(0, 4, accumulate, (jnp.zeros((2 * HEADS, 128), f32), jnp.zeros((128, 2 * HEADS), f32)))
    dest_s[...] = (64.0 * d[:HEADS] + d[HEADS:]).astype(i32)
    destt_s[...] = (64.0 * dt[:, :HEADS] + dt[:, HEADS:]).astype(i32)

    def build(group):
        for slot in range(SLOTS):
            row = dest_s[pl.ds(at_distance(group, slot, -1), 1), :]

            def block_of(kb, _):
                base = pl.multiple_of(kb * 256, 256)
                onehot[group, pl.ds(base, 256), slot * 128:(slot + 1) * 128] = as_mask(
                    iota((256, 128), 0) + base == row)
                return 0

            lax.fori_loop(0, LIST // 256, block_of, 0)

    def tables():
        listed = jnp.zeros((128, 128), f32)
        for r in range(REPS):
            for group in range(GROUPS):
                listed = listed + product(
                    as_mask((owner == r) & (second == group)), as_mask(cols == r * GROUPS + group))
        pair = as_mask((iota((CLUSTERS, 128), 1) >> 1) == iota((CLUSTERS, 128), 0))
        counts = product(pair, listed.astype(bf16))
        before = as_mask(iota((CLUSTERS, CLUSTERS), 1) < iota((CLUSTERS, CLUSTERS), 0))
        offsets = product(before, counts.astype(bf16))
        table_s[0:CLUSTERS, :] = counts.astype(i32)
        table_s[CLUSTERS:2 * CLUSTERS, :] = offsets.astype(i32)
        c_row, c_col = iota((CLUSTERS, CLUSTERS), 1), iota((CLUSTERS, CLUSTERS), 0)
        ext_row = ext_ref[...]
        ext_col = dot_nt(as_mask(c_row == c_col), jnp.broadcast_to(ext_row, (8, CLUSTERS)).astype(f32).astype(bf16))
        ext_col = ext_col[:, 0:1].astype(i32)
        earlier = (ext_row < ext_col) | ((ext_row == ext_col) & (c_row < c_col))
        place = jnp.sum(jnp.where(earlier, 1.0, 0.0), axis=1, keepdims=True).astype(i32)
        hit = as_mask(place == iota((CLUSTERS, 128), 1))
        table_s[2 * CLUSTERS:2 * CLUSTERS + 8, :] = product(
            iota((8, CLUSTERS), 1).astype(f32).astype(bf16), hit).astype(i32)

    def wait_in(a, group):
        def one(slot, _):
            a2a_copy(a, group, slot).wait_recv()
            return 0

        lax.fori_loop(1 - group, SLOTS, one, 0)
        if group == 0:
            own_copy(a).wait()

    def rows_of(c):
        return pl.ds(pl.multiple_of(c * CHUNK, CHUNK), CHUNK)

    def ycopy(a, kind, c):
        if kind == 0:
            src, slot, to = sorted_.at[a, rows_of(c)], rep, right
        elif kind == 1:
            src, slot, to = sorted_.at[a, rows_of(c)], rep, left
        else:
            even = lax.rem(c, 2) == 0
            slot = jnp.where(even, left, right)
            to = jnp.where(even, right, left)
            src = alls[a].at[slot, rows_of(c)]
        return pltpu.make_async_remote_copy(
            src_ref=src, dst_ref=alls[a].at[slot, rows_of(c)],
            send_sem=ysend.at[a, kind, c], recv_sem=yrecv.at[a, kind, c],
            device_id={"rep": to}, device_id_type=MESH)

    def keep_copy(a, c):
        to = alls[a].at[rep, rows_of(c)] if a < 2 else qs.at[rows_of(c)]
        return pltpu.make_async_copy(sorted_.at[a, rows_of(c)], to, keep_sem.at[a, c])

    def wait_y(a, kind, c):
        slot = (left, right, lax.rem(rep + 2, REPS))[kind]
        pltpu.make_async_remote_copy(
            src_ref=sorted_.at[a, rows_of(c)], dst_ref=alls[a].at[slot, rows_of(c)],
            send_sem=ysend.at[a, kind, c], recv_sem=yrecv.at[a, kind, c],
            device_id={"rep": right}, device_id_type=MESH).wait_recv()

    per_group = CHUNKS // GROUPS
    table_copy = pltpu.make_async_copy(table_s, table_out, out_sem.at[0])
    destt_copy = pltpu.make_async_copy(destt_s, destt_out, out_sem.at[1])
    for a in range(3):
        for group in range(GROUPS):
            if a == 0:
                build(group)
            wait_in(a, group)

            def sort(i, _):
                c = group * per_group + i
                sorted_[a, rows_of(c)] = jnp.dot(
                    onehot[group, rows_of(i), :], rx[a, group], preferred_element_type=f32).astype(bf16)
                if a < 2:
                    ycopy(a, 0, c).start()
                    ycopy(a, 1, c).start()
                keep_copy(a, c).start()
                return 0

            lax.fori_loop(0, per_group, sort, 0)
            if a == 0 and group == 0:
                tables()
                table_copy.start()
                destt_copy.start()
            if a < 2:
                def forward(i, _):
                    c = group * per_group + i
                    wait_y(a, 0, c)
                    wait_y(a, 1, c)
                    ycopy(a, 2, c).start()
                    return 0

                lax.fori_loop(0, per_group, forward, 0)

    table_copy.wait()
    destt_copy.wait()

    def finish(c, _):
        for a in range(3):
            keep_copy(a, c).wait()
        for a in range(2):
            wait_y(a, 2, c)
            for kind in range(3):
                ycopy(a, kind, c).wait_send()
        return 0

    lax.fori_loop(0, CHUNKS, finish, 0)

    for a in range(3):
        for group in range(GROUPS):
            def sent(slot, _):
                a2a_copy(a, group, slot).wait_send()
                return 0

            lax.fori_loop(1 - group, SLOTS, sent, 0)


def gather_call(q, k, v, order, ext):
    any_ = pl.BlockSpec(memory_space=pl.ANY)
    vmem = pl.BlockSpec(memory_space=pltpu.VMEM)
    return pl.pallas_call(
        gather_kernel,
        out_shape=(
            jax.ShapeDtypeStruct((REPS, SPAN, DIM), bf16),
            jax.ShapeDtypeStruct((REPS, SPAN, DIM), bf16),
            jax.ShapeDtypeStruct((SPAN, DIM), bf16),
            jax.ShapeDtypeStruct((2 * CLUSTERS + 8, 128), i32),
            jax.ShapeDtypeStruct((LOCAL, HEADS), i32),
        ),
        in_specs=[any_, any_, any_, any_, vmem],
        out_specs=(any_,) * 5,
        scratch_shapes=[
            pltpu.VMEM((3, GROUPS, LIST, DIM), bf16),
            pltpu.VMEM((3, SPAN, DIM), bf16),
            pltpu.VMEM((GROUPS, LIST, LIST), bf16),
            pltpu.VMEM((128, 128), i32),
            pltpu.VMEM((128, 128), i32),
            pltpu.VMEM((128, 128), i32),
            pltpu.VMEM((4, 128, 128), f32),
            pltpu.VMEM((HEADS, LOCAL), i32),
            pltpu.VMEM((LOCAL, HEADS), i32),
            pltpu.VMEM((2 * CLUSTERS + 8, 128), i32),
            pltpu.SemaphoreType.DMA((3, GROUPS, SLOTS)),
            pltpu.SemaphoreType.DMA((3, GROUPS, SLOTS)),
            pltpu.SemaphoreType.DMA((3,)),
            pltpu.SemaphoreType.DMA((128,)),
            pltpu.SemaphoreType.DMA((2, 3, CHUNKS)),
            pltpu.SemaphoreType.DMA((2, 3, CHUNKS)),
            pltpu.SemaphoreType.DMA((3, CHUNKS)),
            pltpu.SemaphoreType.DMA((2,)),
        ],
        compiler_params=pltpu.CompilerParams(
            collective_id=0, has_side_effects=True, vmem_limit_bytes=56 * 2**20),
        name="gather_sorted",
    )(q, k, v, order, ext)


GROUP = 4


def attend_kernel(table, list_ref, ext_ref, rep_ref, kall, vall, qs, out, kc, vc, acc):
    ones = jnp.ones((CLUSTER, DIM), bf16)
    rep = rep_ref[0]

    def span(c):
        return pl.ds(pl.multiple_of(c * CLUSTER, CLUSTER), CLUSTER)

    def extent_of(c, r, group):
        return table[CLUSTERS + c, r * GROUPS + group], table[c, r * GROUPS + group]

    def picked(c, r, k, start):
        lane = iota((1, 128), 1)
        ats, shifts, lows, highs = [], [], [], []
        for group in range(GROUPS):
            off, n = extent_of(c, r, group)
            lo = (off // 16) * 16 + k * WINDOW
            at = jnp.minimum(lo, LIST - WINDOW)
            first = start + jnp.maximum(lo - off, 0)
            last = start + jnp.minimum(n, lo + WINDOW - off)
            ats.append(pl.multiple_of(at, 16))
            shifts.append(start + at - off - group * WINDOW)
            lows.append(first)
            highs.append(last)
            start = start + n
        is_first = lane < WINDOW
        place = lane + jnp.where(is_first, shifts[0], shifts[1])
        inside = (place >= jnp.where(is_first, lows[0], lows[1])) & (place < jnp.where(is_first, highs[0], highs[1]))
        return ats, jnp.where(inside, place, -1), start

    def windows_of(ref, ats, r):
        return [ref[r, pl.ds(ats[g] + g * LIST, WINDOW), :] for g in range(GROUPS)]

    def hot(place, rows, base=0):
        return jnp.where(iota((rows, 128), 0) + base == place, 1.0, 0.0).astype(bf16)

    def join(c, k):
        start = jnp.int32(0)
        hots, keys, vals = [], [], []
        for r in range(REPS):
            ats, place, start = picked(c, r, k, start)
            hots.append(hot(place, CLUSTER))
            keys += windows_of(kall, ats, r)
            vals += windows_of(vall, ats, r)
        kv = jnp.concatenate([jnp.concatenate(keys, 0), jnp.concatenate(vals, 0)], 1)
        return jnp.dot(jnp.concatenate(hots, 1), kv, preferred_element_type=f32)

    def store(c, whole):
        kc[span(c), :] = whole[:, :DIM].astype(bf16)
        vc[span(c), :] = jnp.concatenate([whole[:, DIM:].astype(bf16), ones], 1)

    def rounds(c, r):
        most = jnp.int32(0)
        for group in range(GROUPS):
            off, n = extent_of(c, r, group)
            most = jnp.maximum(most, off % 16 + n)
        return (most + WINDOW - 1) // WINDOW

    def compact(i, _):
        cs = [i * GROUP + u for u in range(GROUP)]
        for c in cs:
            store(c, join(c, 0))
        for c in cs:
            most = functools.reduce(jnp.maximum, [rounds(c, r) for r in range(REPS)])

            @pl.when(most > 1)
            def _():
                store(c, lax.fori_loop(0, most, lambda k, whole: whole + join(c, k),
                                       jnp.zeros((CLUSTER, 2 * DIM), f32)))
        return 0

    lax.fori_loop(0, CLUSTERS // GROUP, compact, 0)

    factor = DIM ** -0.5 * 1.4426950408889634

    def queries_of(c):
        off0, n0 = extent_of(c, rep, 0)
        off1, n1 = extent_of(c, rep, 1)
        return off0 + off1, n0 + n1

    def pick_queries(c, at, off, k):
        ats, place, _ = picked(c, rep, k, off)
        rows = [qs[pl.ds(ats[g] + g * LIST, WINDOW), :] for g in range(GROUPS)]
        return jnp.dot(hot(place, QROWS, at), jnp.concatenate(rows, 0), preferred_element_type=f32)

    def attend_rows(cs, k, size, slow):
        rows, live, blocks, tops, scores, queries = [], [], [], [], [], []
        for c in cs:
            off, n = queries_of(c)
            lo = (off // 16) * 16 + k * QROWS
            at = jnp.minimum(lo, SPAN - QROWS)
            rows.append(pl.ds(pl.multiple_of(at, 16), QROWS))
            row = iota((QROWS, DIM), 0) + at
            live.append((row >= jnp.maximum(off, lo)) & (row < jnp.minimum(off + n, lo + QROWS)))
            blocks.append([span(list_ref[c, jnp.where(j < ext_ref[c], j, 0)]) for j in range(size)])
            if slow:
                query = lax.fori_loop(0, rounds(c, rep), lambda i, q: q + pick_queries(c, at, off, i),
                                      jnp.zeros((QROWS, DIM), f32))
            else:
                query = pick_queries(c, at, off, 0)
            queries.append(query.astype(bf16))
        for u in range(len(cs)):
            scores.append([dot_nt(queries[u], kc[b, :]) for b in blocks[u]])
        for u in range(len(cs)):
            tops.append(jnp.max(functools.reduce(jnp.maximum, scores[u]), axis=1, keepdims=True))
        results = []
        for u, c in enumerate(cs):
            mixed = None
            for j in range(size):
                top = tops[u] if j == 0 else jnp.where(j < ext_ref[c], tops[u], jnp.inf)
                power = jnp.exp2((scores[u][j] - top) * factor).astype(bf16)
                part = jnp.dot(power, vc[blocks[u][j], :], preferred_element_type=f32)
                mixed = part if mixed is None else mixed + part
            results.append(mixed[:, :DIM] / mixed[:, DIM:])
        for u in range(len(cs)):
            acc[rows[u], :] = jnp.where(live[u], results[u], acc[rows[u], :])

    def attend(g, _):
        cs = [table[2 * CLUSTERS, g * GROUP + u] for u in range(GROUP)]
        size_most = ext_ref[cs[-1]]
        for size in range(1, 9):
            @pl.when(size_most == size)
            def _():
                attend_rows(cs, 0, size, False)
        for c in cs:
            off, n = queries_of(c)

            def more(k, _):
                attend_rows([c], k, 8, True)
                return 0

            lax.fori_loop(jnp.where(rounds(c, rep) > 1, 0, 1), (off % 16 + n + QROWS - 1) // QROWS, more, 0)
        return 0

    lax.fori_loop(0, CLUSTERS // GROUP, attend, 0)

    def finish(i, _):
        rows = pl.ds(pl.multiple_of(i * 512, 512), 512)
        out[rows, :] = acc[rows, :].astype(bf16)
        return 0

    lax.fori_loop(0, SPAN // 512, finish, 0)


def attend_call(table, listed, ext, rep, kall, vall, qs):
    smem = pl.BlockSpec(memory_space=pltpu.SMEM)
    vmem = pl.BlockSpec(memory_space=pltpu.VMEM)
    return pl.pallas_call(
        attend_kernel,
        out_shape=jax.ShapeDtypeStruct((SPAN, DIM), bf16),
        in_specs=[smem] * 4 + [vmem] * 3,
        out_specs=vmem,
        scratch_shapes=[
            pltpu.VMEM((TOKENS, DIM), bf16),
            pltpu.VMEM((TOKENS, 2 * DIM), bf16),
            pltpu.VMEM((SPAN, DIM), f32),
        ],
        compiler_params=pltpu.CompilerParams(vmem_limit_bytes=56 * 2**20),
        name="attend",
    )(table, listed, ext, rep, kall, vall, qs)


HALF = HEADS // 2


def return_kernel(mixed, destt_ref, out, partner_s, both_s, onehot, tx, swap_send, swap_recv,
                  send_sem, recv_sem, own_sem):
    guide, me = lax.axis_index("guide"), lax.axis_index("seq")
    other = 1 - guide
    head_guide, head_col = me // HALF, me % HALF

    barrier = pltpu.get_barrier_semaphore()
    pl.semaphore_signal(barrier, inc=1, device_id={"guide": other}, device_id_type=MESH)

    def greet(step, _):
        i = lax.rem(head_col + step, HALF)
        pl.semaphore_signal(barrier, inc=1, device_id={"guide": head_guide, "seq": guide * HALF + i},
                            device_id_type=MESH)
        return 0

    lax.fori_loop(1, HALF, greet, 0)

    @pl.when(head_guide != guide)
    def _():
        greet(0, 0)
        pl.semaphore_wait(barrier, HALF + 1)

    @pl.when(head_guide == guide)
    def _():
        pl.semaphore_wait(barrier, HALF)

    swap = pltpu.make_async_remote_copy(
        src_ref=mixed, dst_ref=partner_s, send_sem=swap_send, recv_sem=swap_recv,
        device_id={"guide": other}, device_id_type=MESH)
    swap.start()

    destt = destt_ref[...]
    picked = jnp.where(guide == 0, destt[:, :HALF], destt[:, HALF:])
    for i in range(HALF):
        for c in range(SPAN // 512):
            onehot[i * LOCAL:(i + 1) * LOCAL, c * 512:(c + 1) * 512] = jnp.where(
                picked[:, i:i + 1] == iota((LOCAL, 512), 1) + c * 512, 1.0, 0.0).astype(bf16)
    swap.wait()

    def combine(c, _):
        rows = pl.ds(pl.multiple_of(c * 512, 512), 512)
        own = mixed[rows, :].astype(f32)
        far = partner_s[rows, :].astype(f32)
        conditioned = jnp.where(guide == 0, own, far)
        unconditioned = jnp.where(guide == 0, far, own)
        both_s[rows, :] = (unconditioned + GUIDE_SCALE * (conditioned - unconditioned)).astype(bf16)
        return 0

    lax.fori_loop(0, SPAN // 512, combine, 0)

    def place(col):
        return out.at[:, pl.ds(pl.multiple_of(col * DIM, DIM), DIM)]

    def send_copy(i):
        return pltpu.make_async_remote_copy(
            src_ref=tx.at[i], dst_ref=place(head_col), send_sem=send_sem.at[i],
            recv_sem=recv_sem.at[head_col],
            device_id={"guide": head_guide, "seq": guide * HALF + i}, device_id_type=MESH)

    def wait_copy(col):
        return pltpu.make_async_remote_copy(
            src_ref=tx.at[col], dst_ref=place(col), send_sem=send_sem.at[col],
            recv_sem=recv_sem.at[col], device_id={"guide": other}, device_id_type=MESH)

    own_copy = pltpu.make_async_copy(tx.at[head_col], place(head_col), own_sem)

    def restore(i):
        rows = pl.ds(pl.multiple_of(i * LOCAL, LOCAL), LOCAL)
        tx[i] = jnp.dot(onehot[rows, :], both_s[...], preferred_element_type=f32).astype(bf16)

    def step(j, _):
        i = lax.rem(head_col + j, HALF)
        restore(i)
        send_copy(i).start()
        return 0

    lax.fori_loop(1, HALF, step, 0)
    restore(head_col)

    @pl.when(head_guide == guide)
    def _():
        own_copy.start()

    @pl.when(head_guide != guide)
    def _():
        send_copy(head_col).start()

    def finish(j, _):
        i = lax.rem(head_col + j, HALF)
        send_copy(i).wait_send()
        wait_copy(i).wait_recv()
        return 0

    lax.fori_loop(1, HALF, finish, 0)

    @pl.when(head_guide == guide)
    def _():
        own_copy.wait()

    @pl.when(head_guide != guide)
    def _():
        send_copy(head_col).wait_send()
        wait_copy(head_col).wait_recv()


def return_call(mixed, destt):
    vmem = pl.BlockSpec(memory_space=pltpu.VMEM)
    return pl.pallas_call(
        return_kernel,
        out_shape=jax.ShapeDtypeStruct((LOCAL, HALF * DIM), bf16),
        in_specs=[vmem, vmem],
        out_specs=pl.BlockSpec(memory_space=pl.ANY),
        scratch_shapes=[
            pltpu.VMEM((SPAN, DIM), bf16),
            pltpu.VMEM((SPAN, DIM), bf16),
            pltpu.VMEM((SPAN // 2, SPAN), bf16),
            pltpu.VMEM((HALF, LOCAL, DIM), bf16),
            pltpu.SemaphoreType.DMA,
            pltpu.SemaphoreType.DMA,
            pltpu.SemaphoreType.DMA((HALF,)),
            pltpu.SemaphoreType.DMA((HALF,)),
            pltpu.SemaphoreType.DMA,
        ],
        compiler_params=pltpu.CompilerParams(
            collective_id=1, has_side_effects=True, vmem_limit_bytes=48 * 2**20),
        name="return_tokens",
    )(mixed, destt)


def on_device(queries, key_vectors, value_vectors, cluster_order, key_blocks, extents):
    kall, vall, qs, table, destt = gather_call(
        queries[0], key_vectors[0], value_vectors[0], cluster_order, extents)
    rep = lax.axis_index("rep").astype(i32).reshape(1)
    mixed = attend_call(table, key_blocks[0], extents[0], rep, kall, vall, qs)
    return return_call(mixed, destt)


def solution(mesh):
    placed = (
        P("guide", ("seq", "rep"), None),
        P("guide", ("seq", "rep"), None),
        P("guide", ("seq", "rep"), None),
        P("seq", None),
        P("seq", None, None),
        P("seq", None),
    )
    return jax.shard_map(
        on_device, mesh=mesh, in_specs=placed, out_specs=P(("seq", "rep"), "guide"), check_vma=False
    )
```

```python
import functools

import jax
import jax.numpy as jnp
from jax import lax
from jax.experimental import pallas as pl
from jax.experimental.pallas import tpu as pltpu
from jax.sharding import PartitionSpec as P

MESH = pl.DeviceIdType.MESH
CLUSTER = 256
GUIDE_SCALE = 5.0
HEADS = 32
SEQ_X, SEQ_Z = 4, 8
REPS = 4
TOKENS = 16384
DIM = 128
SPAN = TOKENS // REPS
LOCAL = 128
CLUSTERS = TOKENS // CLUSTER
CHUNK = 512
CHUNKS = SPAN // CHUNK
GROUPS = 2
SLOTS = HEADS // GROUPS
LIST = SPAN // GROUPS
WINDOW = 64
LISTS = REPS * GROUPS
T_OVER, T_OFF_Q, T_N_Q, T_AT_Q, T_OVER_Q, T_WINDOWS_Q, T_PERM = range(LISTS, LISTS + 7)
T_N, T_OFF = 2 * LISTS, 3 * LISTS
QROWS = 96
f32, bf16, i32 = jnp.float32, jnp.bfloat16, jnp.int32

NT = (((1,), (1,)), ((), ()))


def dot_nt(a, b):
    return lax.dot_general(a, b, NT, preferred_element_type=f32)


def iota(shape, dim):
    return lax.broadcasted_iota(i32, shape, dim)


def z_distance(group, i):
    return i + (i // 2) * 2 + (i // 3) * 2 if group == 0 else i + 2 + i // 2


def fill_tables(n, off, start, ext_row, rep, table, place):
    lane = iota((CLUSTERS, 128), 1)
    is_list = lane < LISTS
    at = jnp.minimum((off >> 4) << 4, LIST - WINDOW)
    lead = off - at
    over = jnp.where(is_list & (lead + n > WINDOW), 1, 0)
    own = is_list & ((lane >> 1) == rep)

    def total(a, hit):
        return jnp.sum(jnp.where(hit, a, 0).astype(f32), axis=1, keepdims=True).astype(i32)

    off_q, n_q = total(off, own), total(n, own)
    at_q = jnp.minimum((off_q >> 4) << 4, SPAN - QROWS)
    windows_q = ((off_q & 15) + n_q + QROWS - 1) // QROWS
    first = lane < WINDOW

    def both(a, r):
        return jnp.where(first, a[:, 2 * r:2 * r + 1], a[:, 2 * r + 1:2 * r + 2])

    chosen = jnp.full((CLUSTERS, 128), -1, i32)
    for r in range(REPS):
        start_r = both(start, r)
        spot = lane - jnp.where(first, 0, WINDOW) + start_r - both(lead, r)
        inside = (spot >= start_r) & (spot < start_r + both(n, r))
        place[r] = jnp.where(inside, spot, -1)
        queries = spot - start[:, 2 * r:2 * r + 1] + off_q - at_q
        chosen = jnp.where(rep == r, jnp.where(inside, queries, -1), chosen)
    place[REPS] = chosen

    c_row, c_col = iota((CLUSTERS, CLUSTERS), 1), iota((CLUSTERS, CLUSTERS), 0)
    diagonal = jnp.where(c_row == c_col, 1.0, 0.0).astype(bf16)
    ext_col = dot_nt(diagonal, jnp.broadcast_to(ext_row, (8, CLUSTERS)).astype(f32).astype(bf16))[:, 0:1].astype(i32)
    earlier = (ext_col < ext_row) | ((ext_col == ext_row) & (c_col < c_row))
    rank = jnp.sum(jnp.where(earlier, 1.0, 0.0), axis=0, keepdims=True).astype(i32)
    perm = jnp.sum(jnp.where(rank == c_col, c_row.astype(f32), 0.0), axis=1, keepdims=True).astype(i32)

    fields = jnp.where(is_list, at + (lane & 1) * LIST, 0)
    for field, value in ((T_OVER, total(over, is_list)), (T_OFF_Q, off_q), (T_N_Q, n_q), (T_AT_Q, at_q),
                         (T_OVER_Q, total(over, own)), (T_WINDOWS_Q, windows_q), (T_PERM, perm)):
        fields = jnp.where(lane == field, value, fields)
    for j in range(LISTS):
        fields = jnp.where(lane == T_N + j, n[:, j:j + 1], fields)
        fields = jnp.where(lane == T_OFF + j, off[:, j:j + 1], fields)
    table[...] = fields


def gather_kernel(q_in, k_in, v_in, order_in, ext_ref, kall, vall, qs, table_out, place_out, destt_out,
                  rx, sorted_, onehot, order_s, key_s, low_s, rank_s, dest_s, destt_s, table_s, place_s,
                  send_sem, recv_sem, own_sem, order_sem, ysend, yrecv, keep_sem, out_sem):
    me = lax.axis_index("seq")
    rep = lax.axis_index("rep")
    x, z = me // SEQ_Z, me % SEQ_Z
    right, left = lax.rem(rep + 1, REPS), lax.rem(rep + REPS - 1, REPS)
    ins = (k_in, v_in, q_in)
    alls = (kall, vall)

    def at_distance(group, slot, sign):
        dx, dz = slot // 4, z_distance(group, slot % 4)
        return lax.rem(x + sign * dx + SEQ_X, SEQ_X) * SEQ_Z + lax.rem(z + sign * dz + SEQ_Z, SEQ_Z)

    def order_copy(u):
        return pltpu.make_async_copy(
            order_in.at[:, pl.ds(pl.multiple_of(u * 128, 128), 128)], order_s.at[pl.ds(u, 1), :], order_sem.at[u])

    def fetch(u, _):
        order_copy(u).start()
        return 0

    lax.fori_loop(0, 128, fetch, 0)

    barrier = pltpu.get_barrier_semaphore()
    for group in range(GROUPS):
        def greet(slot, _):
            pl.semaphore_signal(barrier, inc=1, device_id={"seq": at_distance(group, slot, 1)}, device_id_type=MESH)
            return 0

        lax.fori_loop(1 - group, SLOTS, greet, 0)
    pl.semaphore_signal(barrier, inc=1, device_id={"rep": right}, device_id_type=MESH)
    pl.semaphore_signal(barrier, inc=1, device_id={"rep": left}, device_id_type=MESH)
    pl.semaphore_wait(barrier, HEADS - 1 + 2)

    def a2a_copy(a, group, slot):
        peer = at_distance(group, slot, 1)
        return pltpu.make_async_remote_copy(
            src_ref=ins[a].at[:, pl.ds(pl.multiple_of(peer * DIM, DIM), DIM)],
            dst_ref=rx.at[a, group, pl.ds(pl.multiple_of(slot * LOCAL, LOCAL), LOCAL)],
            send_sem=send_sem.at[a, group, slot], recv_sem=recv_sem.at[a, group, slot],
            device_id={"seq": peer}, device_id_type=MESH)

    def own_copy(a):
        return pltpu.make_async_copy(
            ins[a].at[:, pl.ds(pl.multiple_of(me * DIM, DIM), DIM)], rx.at[a, 0, pl.ds(0, LOCAL)], own_sem.at[a])

    for a in range(3):
        own_copy(a).start()
        for group in range(GROUPS):
            def send(slot, _):
                a2a_copy(a, group, slot).start()
                return 0

            lax.fori_loop(1 - group, SLOTS, send, 0)

    def fetched(u, _):
        order_copy(u).wait()
        return 0

    lax.fori_loop(0, 128, fetched, 0)

    order = order_s[...]
    block = order >> 7
    owner = block & (REPS - 1)
    away = (z - (block >> 2)) & (SEQ_Z - 1)
    second = jnp.where((away == 0) | (away == 1) | (away == 4) | (away == 7), 0, 1)
    mine = owner == rep
    rows, cols = iota((128, 128), 0), iota((128, 128), 1)
    as_mask = lambda hit: jnp.where(hit, 1.0, 0.0).astype(bf16)
    product = lambda a, b: jnp.dot(a, b, preferred_element_type=f32)
    upper, lower = as_mask(rows < cols), as_mask(cols < rows)
    to_cluster, past_cluster = as_mask(cols < (rows >> 1) * 2), as_mask(cols < (rows >> 1) * 2 + 2)
    ones = jnp.ones((128, 128), bf16)
    ranks, befores, pasts = [], [], []
    for group in range(GROUPS):
        present = as_mask(mine & (second == group))
        totals = product(present, ones).astype(bf16)
        ranks.append(product(present, upper) + product(lower, totals))
        befores.append(product(to_cluster, totals))
        pasts.append(product(past_cluster, totals))
    rank = jnp.where(second == 0, ranks[0], ranks[1])
    whole = jnp.where(second == 0, ranks[0] + befores[1], ranks[1] + pasts[0])
    rank_hi, whole_hi = jnp.floor(rank * (1.0 / 64.0)), jnp.floor(whole * (1.0 / 64.0))
    key_s[...] = jnp.where(mine, block >> 2, -1)
    low_s[...] = order & (LOCAL - 1)
    rank_s[0] = rank_hi
    rank_s[1] = rank - 64.0 * rank_hi
    rank_s[2] = whole_hi
    rank_s[3] = whole - 64.0 * whole_hi

    def accumulate(step, carry):
        d, dt = carry
        parts, bs = [[], [], [], []], []
        base = pl.multiple_of(step * 32, 32)
        key8, low8 = key_s[pl.ds(base, 32), :], low_s[pl.ds(base, 32), :]
        rank8 = [rank_s[i, pl.ds(base, 32), :] for i in range(4)]
        for j in range(32):
            hit = iota((HEADS, 128), 0) == key8[j:j + 1]
            for i in range(4):
                parts[i].append(jnp.where(hit, rank8[i][j:j + 1], 0.0).astype(bf16))
            bs.append(as_mask(iota((128, 128), 0) == low8[j:j + 1]))
        parts = [jnp.concatenate(p, 1) for p in parts]
        right_m = jnp.concatenate(bs, 1)
        d = d + dot_nt(jnp.concatenate(parts[:2], 0), right_m)
        dt = dt + dot_nt(right_m, jnp.concatenate(parts[2:], 0))
        return d, dt

    d, dt = lax.fori_loop(0, 4, accumulate, (jnp.zeros((2 * HEADS, 128), f32), jnp.zeros((128, 2 * HEADS), f32)))
    dest_s[...] = (64.0 * d[:HEADS] + d[HEADS:]).astype(i32)
    destt_s[...] = (64.0 * dt[:, :HEADS] + dt[:, HEADS:]).astype(i32)

    def build(group):
        for slot in range(SLOTS):
            row = dest_s[pl.ds(at_distance(group, slot, -1), 1), :]

            def block_of(kb, _):
                base = pl.multiple_of(kb * 256, 256)
                onehot[group, pl.ds(base, 256), slot * 128:(slot + 1) * 128] = as_mask(
                    iota((256, 128), 0) + base == row)
                return 0

            lax.fori_loop(0, LIST // 256, block_of, 0)

    def tables():
        listed = jnp.zeros((128, 128), f32)
        for r in range(REPS):
            for group in range(GROUPS):
                listed = listed + product(
                    as_mask((owner == r) & (second == group)), as_mask(cols == r * GROUPS + group))
        pair = as_mask((iota((CLUSTERS, 128), 1) >> 1) == iota((CLUSTERS, 128), 0))
        counts = product(pair, listed.astype(bf16)).astype(bf16)
        before = as_mask(iota((CLUSTERS, CLUSTERS), 1) < iota((CLUSTERS, CLUSTERS), 0))
        offsets = product(before, counts)
        starts = product(counts, upper)
        fill_tables(counts.astype(f32).astype(i32), offsets.astype(i32), starts.astype(i32), ext_ref[...], rep,
                    table_s, place_s)

    def wait_in(a, group):
        def one(slot, _):
            a2a_copy(a, group, slot).wait_recv()
            return 0

        lax.fori_loop(1 - group, SLOTS, one, 0)
        if group == 0:
            own_copy(a).wait()

    def rows_of(c):
        return pl.ds(pl.multiple_of(c * CHUNK, CHUNK), CHUNK)

    def ycopy(a, kind, c):
        if kind == 0:
            src, slot, to = sorted_.at[a, rows_of(c)], rep, right
        elif kind == 1:
            src, slot, to = sorted_.at[a, rows_of(c)], rep, left
        else:
            even = lax.rem(c, 2) == 0
            slot = jnp.where(even, left, right)
            to = jnp.where(even, right, left)
            src = alls[a].at[slot, rows_of(c)]
        return pltpu.make_async_remote_copy(
            src_ref=src, dst_ref=alls[a].at[slot, rows_of(c)],
            send_sem=ysend.at[a, kind, c], recv_sem=yrecv.at[a, kind, c],
            device_id={"rep": to}, device_id_type=MESH)

    def keep_copy(a, c):
        to = alls[a].at[rep, rows_of(c)] if a < 2 else qs.at[rows_of(c)]
        return pltpu.make_async_copy(sorted_.at[a, rows_of(c)], to, keep_sem.at[a, c])

    def wait_y(a, kind, c):
        slot = (left, right, lax.rem(rep + 2, REPS))[kind]
        pltpu.make_async_remote_copy(
            src_ref=sorted_.at[a, rows_of(c)], dst_ref=alls[a].at[slot, rows_of(c)],
            send_sem=ysend.at[a, kind, c], recv_sem=yrecv.at[a, kind, c],
            device_id={"rep": right}, device_id_type=MESH).wait_recv()

    per_group = CHUNKS // GROUPS
    table_copy = pltpu.make_async_copy(table_s, table_out, out_sem.at[0])
    destt_copy = pltpu.make_async_copy(destt_s, destt_out, out_sem.at[1])
    place_copy = pltpu.make_async_copy(place_s, place_out, out_sem.at[2])
    for a in range(3):
        for group in range(GROUPS):
            if a == 0:
                build(group)
            wait_in(a, group)

            def sort(i, _):
                c = group * per_group + i
                sorted_[a, rows_of(c)] = jnp.dot(
                    onehot[group, rows_of(i), :], rx[a, group], preferred_element_type=f32).astype(bf16)
                if a < 2:
                    ycopy(a, 0, c).start()
                    ycopy(a, 1, c).start()
                keep_copy(a, c).start()
                return 0

            lax.fori_loop(0, per_group, sort, 0)
            if a == 0 and group == 0:
                tables()
                table_copy.start()
                place_copy.start()
                destt_copy.start()
            if a < 2:
                def forward(i, _):
                    c = group * per_group + i
                    wait_y(a, 0, c)
                    wait_y(a, 1, c)
                    ycopy(a, 2, c).start()
                    return 0

                lax.fori_loop(0, per_group, forward, 0)

    table_copy.wait()
    place_copy.wait()
    destt_copy.wait()

    def finish(c, _):
        for a in range(3):
            keep_copy(a, c).wait()
        for a in range(2):
            wait_y(a, 2, c)
            for kind in range(3):
                ycopy(a, kind, c).wait_send()
        return 0

    lax.fori_loop(0, CHUNKS, finish, 0)

    for a in range(3):
        for group in range(GROUPS):
            def sent(slot, _):
                a2a_copy(a, group, slot).wait_send()
                return 0

            lax.fori_loop(1 - group, SLOTS, sent, 0)


def gather_call(q, k, v, order, ext):
    any_ = pl.BlockSpec(memory_space=pl.ANY)
    vmem = pl.BlockSpec(memory_space=pltpu.VMEM)
    return pl.pallas_call(
        gather_kernel,
        out_shape=(
            jax.ShapeDtypeStruct((REPS, SPAN, DIM), bf16),
            jax.ShapeDtypeStruct((REPS, SPAN, DIM), bf16),
            jax.ShapeDtypeStruct((SPAN, DIM), bf16),
            jax.ShapeDtypeStruct((CLUSTERS, 128), i32),
            jax.ShapeDtypeStruct((REPS + 1, CLUSTERS, 128), i32),
            jax.ShapeDtypeStruct((LOCAL, HEADS), i32),
        ),
        in_specs=[any_, any_, any_, any_, vmem],
        out_specs=(any_,) * 6,
        scratch_shapes=[
            pltpu.VMEM((3, GROUPS, LIST, DIM), bf16),
            pltpu.VMEM((3, SPAN, DIM), bf16),
            pltpu.VMEM((GROUPS, LIST, LIST), bf16),
            pltpu.VMEM((128, 128), i32),
            pltpu.VMEM((128, 128), i32),
            pltpu.VMEM((128, 128), i32),
            pltpu.VMEM((4, 128, 128), f32),
            pltpu.VMEM((HEADS, LOCAL), i32),
            pltpu.VMEM((LOCAL, HEADS), i32),
            pltpu.VMEM((CLUSTERS, 128), i32),
            pltpu.VMEM((REPS + 1, CLUSTERS, 128), i32),
            pltpu.SemaphoreType.DMA((3, GROUPS, SLOTS)),
            pltpu.SemaphoreType.DMA((3, GROUPS, SLOTS)),
            pltpu.SemaphoreType.DMA((3,)),
            pltpu.SemaphoreType.DMA((128,)),
            pltpu.SemaphoreType.DMA((2, 3, CHUNKS)),
            pltpu.SemaphoreType.DMA((2, 3, CHUNKS)),
            pltpu.SemaphoreType.DMA((3, CHUNKS)),
            pltpu.SemaphoreType.DMA((3,)),
        ],
        compiler_params=pltpu.CompilerParams(
            collective_id=0, has_side_effects=True, vmem_limit_bytes=56 * 2**20),
        name="gather_sorted",
    )(q, k, v, order, ext)


GROUP = 4


def attend_kernel(table, list_ref, ext_ref, rep_ref, place_ref, kall, vall, qs, out, kc, vc, acc):
    ones = jnp.ones((CLUSTER, DIM), bf16)
    rep = rep_ref[0]

    def span(c):
        return pl.ds(pl.multiple_of(c * CLUSTER, CLUSTER), CLUSTER)

    def extent_of(c, r, group):
        return table[c, T_OFF + r * GROUPS + group], table[c, T_N + r * GROUPS + group]

    def picked(c, r, k, start):
        lane = iota((1, 128), 1)
        ats, shifts, lows, highs = [], [], [], []
        for group in range(GROUPS):
            off, n = extent_of(c, r, group)
            lo = (off // 16) * 16 + k * WINDOW
            at = jnp.minimum(lo, LIST - WINDOW)
            first = start + jnp.maximum(lo - off, 0)
            last = start + jnp.minimum(n, lo + WINDOW - off)
            ats.append(pl.multiple_of(at + group * LIST, 16))
            shifts.append(start + at - off - group * WINDOW)
            lows.append(first)
            highs.append(last)
            start = start + n
        is_first = lane < WINDOW
        place = lane + jnp.where(is_first, shifts[0], shifts[1])
        inside = (place >= jnp.where(is_first, lows[0], lows[1])) & (place < jnp.where(is_first, highs[0], highs[1]))
        return ats, jnp.where(inside, place, -1), start

    def first_windows(c, r):
        return [pl.multiple_of(table[c, r * GROUPS + g], 16) for g in range(GROUPS)]

    def windows_of(ref, ats, r):
        return [ref[r, pl.ds(at, WINDOW), :] for at in ats]

    def hot(place, rows):
        return jnp.where(iota((rows, 128), 0) == place, 1.0, 0.0).astype(bf16)

    def join(c, k):
        start = jnp.int32(0)
        hots, keys, vals = [], [], []
        for r in range(REPS):
            if k is None:
                ats, place = first_windows(c, r), place_ref[r, pl.ds(c, 1), :]
            else:
                ats, place, start = picked(c, r, k, start)
            hots.append(hot(place, CLUSTER))
            keys += windows_of(kall, ats, r)
            vals += windows_of(vall, ats, r)
        kv = jnp.concatenate([jnp.concatenate(keys, 0), jnp.concatenate(vals, 0)], 1)
        return jnp.dot(jnp.concatenate(hots, 1), kv, preferred_element_type=f32)

    def store(c, whole):
        kc[span(c), :] = whole[:, :DIM].astype(bf16)
        vc[span(c), :] = jnp.concatenate([whole[:, DIM:].astype(bf16), ones], 1)

    def rounds(c, r):
        most = jnp.int32(0)
        for group in range(GROUPS):
            off, n = extent_of(c, r, group)
            most = jnp.maximum(most, off % 16 + n)
        return (most + WINDOW - 1) // WINDOW

    def compact(i, _):
        cs = [i * GROUP + u for u in range(GROUP)]
        for c in cs:
            store(c, join(c, None))
        for c in cs:
            @pl.when(table[c, T_OVER] > 0)
            def _():
                most = functools.reduce(jnp.maximum, [rounds(c, r) for r in range(REPS)])
                store(c, lax.fori_loop(0, most, lambda k, whole: whole + join(c, k),
                                       jnp.zeros((CLUSTER, 2 * DIM), f32)))
        return 0

    lax.fori_loop(0, CLUSTERS // GROUP, compact, 0)

    factor = DIM ** -0.5 * 1.4426950408889634

    def pick_queries(c, at, k):
        if k is None:
            ats, place = first_windows(c, rep), place_ref[REPS, pl.ds(c, 1), :]
        else:
            ats, place, _ = picked(c, rep, k, table[c, T_OFF_Q] - at)
        rows = [qs[pl.ds(a, WINDOW), :] for a in ats]
        return jnp.dot(hot(place, QROWS), jnp.concatenate(rows, 0), preferred_element_type=f32)

    def attend_rows(cs, k, size, slow):
        rows, live, blocks, tops, scores, queries = [], [], [], [], [], []
        for c in cs:
            off, n = table[c, T_OFF_Q], table[c, T_N_Q]
            if slow:
                lo = (off // 16) * 16 + k * QROWS
                at = jnp.minimum(lo, SPAN - QROWS)
            else:
                lo, at = 0, table[c, T_AT_Q]
            rows.append(pl.ds(pl.multiple_of(at, 16), QROWS))
            row = iota((QROWS, DIM), 0) + at
            live.append((row >= jnp.maximum(off, lo)) & (row < jnp.minimum(off + n, lo + QROWS)) if slow
                        else (row >= off) & (row < off + n))
            blocks.append([span(list_ref[jnp.where(j < ext_ref[c], j, 0), c]) for j in range(size)])
            if slow:
                query = lax.fori_loop(0, rounds(c, rep), lambda i, q: q + pick_queries(c, at, i),
                                      jnp.zeros((QROWS, DIM), f32))
            else:
                query = pick_queries(c, at, None)
            queries.append(query.astype(bf16))
        for u in range(len(cs)):
            scores.append([dot_nt(queries[u], kc[b, :]) for b in blocks[u]])
        for u in range(len(cs)):
            tops.append(jnp.max(functools.reduce(jnp.maximum, scores[u]), axis=1, keepdims=True))
        results = []
        for u, c in enumerate(cs):
            mixed = None
            for j in range(size):
                top = tops[u] if j == 0 else jnp.where(j < ext_ref[c], tops[u], jnp.inf)
                power = jnp.exp2((scores[u][j] - top) * factor).astype(bf16)
                part = jnp.dot(power, vc[blocks[u][j], :], preferred_element_type=f32)
                mixed = part if mixed is None else mixed + part
            results.append(mixed[:, :DIM] / mixed[:, DIM:])
        for u in range(len(cs)):
            acc[rows[u], :] = jnp.where(live[u], results[u], acc[rows[u], :])

    def attend(g, _):
        cs = [table[g * GROUP + u, T_PERM] for u in range(GROUP)]
        size_most = ext_ref[cs[-1]]
        for size in range(1, 9):
            @pl.when(size_most == size)
            def _():
                attend_rows(cs, 0, size, False)
        for c in cs:
            def more(k, _):
                attend_rows([c], k, 8, True)
                return 0

            lax.fori_loop(jnp.where(table[c, T_OVER_Q] > 0, 0, 1), table[c, T_WINDOWS_Q], more, 0)
        return 0

    lax.fori_loop(0, CLUSTERS // GROUP, attend, 0)

    def finish(i, _):
        rows = pl.ds(pl.multiple_of(i * 512, 512), 512)
        out[rows, :] = acc[rows, :].astype(bf16)
        return 0

    lax.fori_loop(0, SPAN // 512, finish, 0)


def attend_call(table, listed, ext, rep, place, kall, vall, qs):
    smem = pl.BlockSpec(memory_space=pltpu.SMEM)
    vmem = pl.BlockSpec(memory_space=pltpu.VMEM)
    return pl.pallas_call(
        attend_kernel,
        out_shape=jax.ShapeDtypeStruct((SPAN, DIM), bf16),
        in_specs=[smem] * 4 + [vmem] * 4,
        out_specs=vmem,
        scratch_shapes=[
            pltpu.VMEM((TOKENS, DIM), bf16),
            pltpu.VMEM((TOKENS, 2 * DIM), bf16),
            pltpu.VMEM((SPAN, DIM), f32),
        ],
        compiler_params=pltpu.CompilerParams(vmem_limit_bytes=56 * 2**20),
        name="attend",
    )(table, listed, ext, rep, place, kall, vall, qs)


HALF = HEADS // 2


def return_kernel(mixed_in, destt_in, out, mixed, destt_ref, partner_s, both_s, onehot, tx, swap_send, swap_recv,
                  send_sem, recv_sem, own_sem, in_sem):
    guide, me = lax.axis_index("guide"), lax.axis_index("seq")
    other = 1 - guide
    head_guide, head_col = me // HALF, me % HALF
    mixed_copy = pltpu.make_async_copy(mixed_in, mixed, in_sem.at[0])
    destt_copy = pltpu.make_async_copy(destt_in, destt_ref, in_sem.at[1])
    mixed_copy.start()
    destt_copy.start()

    barrier = pltpu.get_barrier_semaphore()
    pl.semaphore_signal(barrier, inc=1, device_id={"guide": other}, device_id_type=MESH)

    def greet(step, _):
        i = lax.rem(head_col + step, HALF)
        pl.semaphore_signal(barrier, inc=1, device_id={"guide": head_guide, "seq": guide * HALF + i},
                            device_id_type=MESH)
        return 0

    lax.fori_loop(1, HALF, greet, 0)

    @pl.when(head_guide != guide)
    def _():
        greet(0, 0)
        pl.semaphore_wait(barrier, HALF + 1)

    @pl.when(head_guide == guide)
    def _():
        pl.semaphore_wait(barrier, HALF)

    swap = pltpu.make_async_remote_copy(
        src_ref=mixed_in, dst_ref=partner_s, send_sem=swap_send, recv_sem=swap_recv,
        device_id={"guide": other}, device_id_type=MESH)
    swap.start()

    destt_copy.wait()
    destt = destt_ref[...]
    picked = jnp.where(guide == 0, destt[:, :HALF], destt[:, HALF:])
    for i in range(HALF):
        for c in range(SPAN // 512):
            onehot[i * LOCAL:(i + 1) * LOCAL, c * 512:(c + 1) * 512] = jnp.where(
                picked[:, i:i + 1] == iota((LOCAL, 512), 1) + c * 512, 1.0, 0.0).astype(bf16)
    mixed_copy.wait()
    swap.wait()

    def combine(c, _):
        rows = pl.ds(pl.multiple_of(c * 512, 512), 512)
        own = mixed[rows, :].astype(f32)
        far = partner_s[rows, :].astype(f32)
        conditioned = jnp.where(guide == 0, own, far)
        unconditioned = jnp.where(guide == 0, far, own)
        both_s[rows, :] = (unconditioned + GUIDE_SCALE * (conditioned - unconditioned)).astype(bf16)
        return 0

    lax.fori_loop(0, SPAN // 512, combine, 0)

    def place(col):
        return out.at[:, pl.ds(pl.multiple_of(col * DIM, DIM), DIM)]

    def send_copy(i):
        return pltpu.make_async_remote_copy(
            src_ref=tx.at[i], dst_ref=place(head_col), send_sem=send_sem.at[i],
            recv_sem=recv_sem.at[head_col],
            device_id={"guide": head_guide, "seq": guide * HALF + i}, device_id_type=MESH)

    def wait_copy(col):
        return pltpu.make_async_remote_copy(
            src_ref=tx.at[col], dst_ref=place(col), send_sem=send_sem.at[col],
            recv_sem=recv_sem.at[col], device_id={"guide": other}, device_id_type=MESH)

    own_copy = pltpu.make_async_copy(tx.at[head_col], place(head_col), own_sem)

    def restore(i):
        rows = pl.ds(pl.multiple_of(i * LOCAL, LOCAL), LOCAL)
        tx[i] = jnp.dot(onehot[rows, :], both_s[...], preferred_element_type=f32).astype(bf16)

    def step(j, _):
        i = lax.rem(head_col + j, HALF)
        restore(i)
        send_copy(i).start()
        return 0

    lax.fori_loop(1, HALF, step, 0)
    restore(head_col)

    @pl.when(head_guide == guide)
    def _():
        own_copy.start()

    @pl.when(head_guide != guide)
    def _():
        send_copy(head_col).start()

    def finish(j, _):
        i = lax.rem(head_col + j, HALF)
        send_copy(i).wait_send()
        wait_copy(i).wait_recv()
        return 0

    lax.fori_loop(1, HALF, finish, 0)

    @pl.when(head_guide == guide)
    def _():
        own_copy.wait()

    @pl.when(head_guide != guide)
    def _():
        send_copy(head_col).wait_send()
        wait_copy(head_col).wait_recv()


def return_call(mixed, destt):
    any_ = pl.BlockSpec(memory_space=pl.ANY)
    return pl.pallas_call(
        return_kernel,
        out_shape=jax.ShapeDtypeStruct((LOCAL, HALF * DIM), bf16),
        in_specs=[any_, any_],
        out_specs=any_,
        scratch_shapes=[
            pltpu.VMEM((SPAN, DIM), bf16),
            pltpu.VMEM((LOCAL, HEADS), i32),
            pltpu.VMEM((SPAN, DIM), bf16),
            pltpu.VMEM((SPAN, DIM), bf16),
            pltpu.VMEM((SPAN // 2, SPAN), bf16),
            pltpu.VMEM((HALF, LOCAL, DIM), bf16),
            pltpu.SemaphoreType.DMA,
            pltpu.SemaphoreType.DMA,
            pltpu.SemaphoreType.DMA((HALF,)),
            pltpu.SemaphoreType.DMA((HALF,)),
            pltpu.SemaphoreType.DMA,
            pltpu.SemaphoreType.DMA((2,)),
        ],
        compiler_params=pltpu.CompilerParams(
            collective_id=1, has_side_effects=True, vmem_limit_bytes=48 * 2**20),
        name="return_tokens",
    )(mixed, destt)


def on_device(queries, key_vectors, value_vectors, cluster_order, key_blocks, extents):
    kall, vall, qs, table, place, destt = gather_call(
        queries[0], key_vectors[0], value_vectors[0], cluster_order, extents)
    rep = lax.axis_index("rep").astype(i32).reshape(1)
    mixed = attend_call(table, key_blocks[0].T, extents[0], rep, place, kall, vall, qs)
    return return_call(mixed, destt)


def solution(mesh):
    placed = (
        P("guide", ("seq", "rep"), None),
        P("guide", ("seq", "rep"), None),
        P("guide", ("seq", "rep"), None),
        P("seq", None),
        P("seq", None, None),
        P("seq", None),
    )
    return jax.shard_map(
        on_device, mesh=mesh, in_specs=placed, out_specs=P(("seq", "rep"), "guide"), check_vma=False
    )
```

```python
import functools

import jax
import jax.numpy as jnp
from jax import lax
from jax.experimental import pallas as pl
from jax.experimental.pallas import tpu as pltpu
from jax.sharding import PartitionSpec as P

MESH = pl.DeviceIdType.MESH
CLUSTER = 256
GUIDE_SCALE = 5.0
HEADS = 32
SEQ_X, SEQ_Z = 4, 8
REPS = 4
TOKENS = 16384
DIM = 128
SPAN = TOKENS // REPS
LOCAL = 128
CLUSTERS = TOKENS // CLUSTER
CHUNK = 512
CHUNKS = SPAN // CHUNK
GROUPS = 2
SLOTS = HEADS // GROUPS
LIST = SPAN // GROUPS
WINDOW = 64
LISTS = REPS * GROUPS
T_OVER, T_OFF_Q, T_N_Q, T_AT_Q, T_OVER_Q, T_WINDOWS_Q, T_PERM = range(LISTS, LISTS + 7)
T_N, T_OFF = 2 * LISTS, 3 * LISTS
QROWS = 96
f32, bf16, i32 = jnp.float32, jnp.bfloat16, jnp.int32

NT = (((1,), (1,)), ((), ()))


def dot_nt(a, b):
    return lax.dot_general(a, b, NT, preferred_element_type=f32)


def iota(shape, dim):
    return lax.broadcasted_iota(i32, shape, dim)


def z_distance(group, dx, i):
    far = 4 * (dx // 2)
    if group == 0:
        return i + (i // 2) * 5 + (i // 3) * (far - 6)
    return i + 2 + (1 - (i + 2) // 3) * (4 - far)


def fill_tables(n, off, start, ext_row, rep, table, place):
    lane = iota((CLUSTERS, 128), 1)
    is_list = lane < LISTS
    at = jnp.minimum((off >> 4) << 4, LIST - WINDOW)
    lead = off - at
    over = jnp.where(is_list & (lead + n > WINDOW), 1, 0)
    own = is_list & ((lane >> 1) == rep)

    def total(a, hit):
        return jnp.sum(jnp.where(hit, a, 0).astype(f32), axis=1, keepdims=True).astype(i32)

    off_q, n_q = total(off, own), total(n, own)
    at_q = jnp.minimum((off_q >> 4) << 4, SPAN - QROWS)
    windows_q = ((off_q & 15) + n_q + QROWS - 1) // QROWS
    first = lane < WINDOW

    def both(a, r):
        return jnp.where(first, a[:, 2 * r:2 * r + 1], a[:, 2 * r + 1:2 * r + 2])

    chosen = jnp.full((CLUSTERS, 128), -1, i32)
    for r in range(REPS):
        start_r = both(start, r)
        spot = lane - jnp.where(first, 0, WINDOW) + start_r - both(lead, r)
        inside = (spot >= start_r) & (spot < start_r + both(n, r))
        place[r] = jnp.where(inside, spot, -1)
        queries = spot - start[:, 2 * r:2 * r + 1] + off_q - at_q
        chosen = jnp.where(rep == r, jnp.where(inside, queries, -1), chosen)
    place[REPS] = chosen

    c_row, c_col = iota((CLUSTERS, CLUSTERS), 1), iota((CLUSTERS, CLUSTERS), 0)
    diagonal = jnp.where(c_row == c_col, 1.0, 0.0).astype(bf16)
    ext_col = dot_nt(diagonal, jnp.broadcast_to(ext_row, (8, CLUSTERS)).astype(f32).astype(bf16))[:, 0:1].astype(i32)
    earlier = (ext_col < ext_row) | ((ext_col == ext_row) & (c_col < c_row))
    rank = jnp.sum(jnp.where(earlier, 1.0, 0.0), axis=0, keepdims=True).astype(i32)
    perm = jnp.sum(jnp.where(rank == c_col, c_row.astype(f32), 0.0), axis=1, keepdims=True).astype(i32)

    fields = jnp.where(is_list, at + (lane & 1) * LIST, 0)
    for field, value in ((T_OVER, total(over, is_list)), (T_OFF_Q, off_q), (T_N_Q, n_q), (T_AT_Q, at_q),
                         (T_OVER_Q, total(over, own)), (T_WINDOWS_Q, windows_q), (T_PERM, perm)):
        fields = jnp.where(lane == field, value, fields)
    for j in range(LISTS):
        fields = jnp.where(lane == T_N + j, n[:, j:j + 1], fields)
        fields = jnp.where(lane == T_OFF + j, off[:, j:j + 1], fields)
    table[...] = fields


def gather_kernel(q_in, k_in, v_in, order_in, ext_ref, kall, vall, qs, table_out, place_out, destt_out,
                  rx, sorted_, onehot, order_s, key_s, low_s, rank_s, dest_s, destt_s, table_s, place_s,
                  send_sem, recv_sem, own_sem, order_sem, ysend, yrecv, keep_sem, out_sem):
    me = lax.axis_index("seq")
    rep = lax.axis_index("rep")
    x, z = me // SEQ_Z, me % SEQ_Z
    right, left = lax.rem(rep + 1, REPS), lax.rem(rep + REPS - 1, REPS)
    ins = (k_in, v_in, q_in)
    alls = (kall, vall)

    def at_distance(group, slot, sign):
        dx = slot // 4
        dz = z_distance(group, dx, slot % 4)
        return lax.rem(x + sign * dx + SEQ_X, SEQ_X) * SEQ_Z + lax.rem(z + sign * dz + SEQ_Z, SEQ_Z)

    def order_copy(u):
        return pltpu.make_async_copy(
            order_in.at[:, pl.ds(pl.multiple_of(u * 128, 128), 128)], order_s.at[pl.ds(u, 1), :], order_sem.at[u])

    def fetch(u, _):
        order_copy(u).start()
        return 0

    lax.fori_loop(0, 128, fetch, 0)

    barrier = pltpu.get_barrier_semaphore()
    for group in range(GROUPS):
        def greet(slot, _):
            pl.semaphore_signal(barrier, inc=1, device_id={"seq": at_distance(group, slot, 1)}, device_id_type=MESH)
            return 0

        lax.fori_loop(1 - group, SLOTS, greet, 0)
    pl.semaphore_signal(barrier, inc=1, device_id={"rep": right}, device_id_type=MESH)
    pl.semaphore_signal(barrier, inc=1, device_id={"rep": left}, device_id_type=MESH)
    pl.semaphore_wait(barrier, HEADS - 1 + 2)

    def a2a_copy(a, group, slot):
        peer = at_distance(group, slot, 1)
        return pltpu.make_async_remote_copy(
            src_ref=ins[a].at[:, pl.ds(pl.multiple_of(peer * DIM, DIM), DIM)],
            dst_ref=rx.at[a, group, pl.ds(pl.multiple_of(slot * LOCAL, LOCAL), LOCAL)],
            send_sem=send_sem.at[a, group, slot], recv_sem=recv_sem.at[a, group, slot],
            device_id={"seq": peer}, device_id_type=MESH)

    def own_copy(a):
        return pltpu.make_async_copy(
            ins[a].at[:, pl.ds(pl.multiple_of(me * DIM, DIM), DIM)], rx.at[a, 0, pl.ds(0, LOCAL)], own_sem.at[a])

    units = ((0, 0), (1, 0), (0, 1), (1, 1), (2, 0), (2, 1))
    for a, group in units:
        if group == 0:
            own_copy(a).start()

        def send(slot, _):
            a2a_copy(a, group, slot).start()
            return 0

        lax.fori_loop(1 - group, SLOTS, send, 0)

    def fetched(u, _):
        order_copy(u).wait()
        return 0

    lax.fori_loop(0, 128, fetched, 0)

    order = order_s[...]
    block = order >> 7
    owner = block & (REPS - 1)
    away_x = (x - (block >> 5)) & (SEQ_X - 1)
    away_z = (z - (block >> 2)) & (SEQ_Z - 1)
    near = (away_z == 0) | (away_z == 1) | (away_z == 7) | (away_z == 2 + 4 * (away_x >> 1))
    second = jnp.where(near, 0, 1)
    mine = owner == rep
    rows, cols = iota((128, 128), 0), iota((128, 128), 1)
    as_mask = lambda hit: jnp.where(hit, 1.0, 0.0).astype(bf16)
    product = lambda a, b: jnp.dot(a, b, preferred_element_type=f32)
    upper, lower = as_mask(rows < cols), as_mask(cols < rows)
    to_cluster, past_cluster = as_mask(cols < (rows >> 1) * 2), as_mask(cols < (rows >> 1) * 2 + 2)
    ones = jnp.ones((128, 128), bf16)
    ranks, befores, pasts = [], [], []
    for group in range(GROUPS):
        present = as_mask(mine & (second == group))
        totals = product(present, ones).astype(bf16)
        ranks.append(product(present, upper) + product(lower, totals))
        befores.append(product(to_cluster, totals))
        pasts.append(product(past_cluster, totals))
    rank = jnp.where(second == 0, ranks[0], ranks[1])
    whole = jnp.where(second == 0, ranks[0] + befores[1], ranks[1] + pasts[0])
    rank_hi, whole_hi = jnp.floor(rank * (1.0 / 64.0)), jnp.floor(whole * (1.0 / 64.0))
    key_s[...] = jnp.where(mine, block >> 2, -1)
    low_s[...] = order & (LOCAL - 1)
    rank_s[0] = rank_hi
    rank_s[1] = rank - 64.0 * rank_hi
    rank_s[2] = whole_hi
    rank_s[3] = whole - 64.0 * whole_hi

    def accumulate(step, carry):
        d, dt = carry
        parts, bs = [[], [], [], []], []
        base = pl.multiple_of(step * 32, 32)
        key8, low8 = key_s[pl.ds(base, 32), :], low_s[pl.ds(base, 32), :]
        rank8 = [rank_s[i, pl.ds(base, 32), :] for i in range(4)]
        for j in range(32):
            hit = iota((HEADS, 128), 0) == key8[j:j + 1]
            for i in range(4):
                parts[i].append(jnp.where(hit, rank8[i][j:j + 1], 0.0).astype(bf16))
            bs.append(as_mask(iota((128, 128), 0) == low8[j:j + 1]))
        parts = [jnp.concatenate(p, 1) for p in parts]
        right_m = jnp.concatenate(bs, 1)
        d = d + dot_nt(jnp.concatenate(parts[:2], 0), right_m)
        dt = dt + dot_nt(right_m, jnp.concatenate(parts[2:], 0))
        return d, dt

    d, dt = lax.fori_loop(0, 4, accumulate, (jnp.zeros((2 * HEADS, 128), f32), jnp.zeros((128, 2 * HEADS), f32)))
    dest_s[...] = (64.0 * d[:HEADS] + d[HEADS:]).astype(i32)
    destt_s[...] = (64.0 * dt[:, :HEADS] + dt[:, HEADS:]).astype(i32)

    def build(group):
        for slot in range(SLOTS):
            row = dest_s[pl.ds(at_distance(group, slot, -1), 1), :]

            def block_of(kb, _):
                base = pl.multiple_of(kb * 256, 256)
                onehot[group, pl.ds(base, 256), slot * 128:(slot + 1) * 128] = as_mask(
                    iota((256, 128), 0) + base == row)
                return 0

            lax.fori_loop(0, LIST // 256, block_of, 0)

    def tables():
        listed = jnp.zeros((128, 128), f32)
        for r in range(REPS):
            for group in range(GROUPS):
                listed = listed + product(
                    as_mask((owner == r) & (second == group)), as_mask(cols == r * GROUPS + group))
        pair = as_mask((iota((CLUSTERS, 128), 1) >> 1) == iota((CLUSTERS, 128), 0))
        counts = product(pair, listed.astype(bf16)).astype(bf16)
        before = as_mask(iota((CLUSTERS, CLUSTERS), 1) < iota((CLUSTERS, CLUSTERS), 0))
        offsets = product(before, counts)
        starts = product(counts, upper)
        fill_tables(counts.astype(f32).astype(i32), offsets.astype(i32), starts.astype(i32), ext_ref[...], rep,
                    table_s, place_s)

    def wait_in(a, group):
        def one(slot, _):
            a2a_copy(a, group, slot).wait_recv()
            return 0

        lax.fori_loop(1 - group, SLOTS, one, 0)
        if group == 0:
            own_copy(a).wait()

    def rows_of(c):
        return pl.ds(pl.multiple_of(c * CHUNK, CHUNK), CHUNK)

    def ycopy(a, kind, c):
        if kind == 0:
            src, slot, to = sorted_.at[a, rows_of(c)], rep, right
        elif kind == 1:
            src, slot, to = sorted_.at[a, rows_of(c)], rep, left
        else:
            even = lax.rem(c, 2) == 0
            slot = jnp.where(even, left, right)
            to = jnp.where(even, right, left)
            src = alls[a].at[slot, rows_of(c)]
        return pltpu.make_async_remote_copy(
            src_ref=src, dst_ref=alls[a].at[slot, rows_of(c)],
            send_sem=ysend.at[a, kind, c], recv_sem=yrecv.at[a, kind, c],
            device_id={"rep": to}, device_id_type=MESH)

    def keep_copy(a, c):
        to = alls[a].at[rep, rows_of(c)] if a < 2 else qs.at[rows_of(c)]
        return pltpu.make_async_copy(sorted_.at[a, rows_of(c)], to, keep_sem.at[a, c])

    def wait_y(a, kind, c):
        slot = (left, right, lax.rem(rep + 2, REPS))[kind]
        pltpu.make_async_remote_copy(
            src_ref=sorted_.at[a, rows_of(c)], dst_ref=alls[a].at[slot, rows_of(c)],
            send_sem=ysend.at[a, kind, c], recv_sem=yrecv.at[a, kind, c],
            device_id={"rep": right}, device_id_type=MESH).wait_recv()

    per_group = CHUNKS // GROUPS
    table_copy = pltpu.make_async_copy(table_s, table_out, out_sem.at[0])
    destt_copy = pltpu.make_async_copy(destt_s, destt_out, out_sem.at[1])
    place_copy = pltpu.make_async_copy(place_s, place_out, out_sem.at[2])
    for a, group in units:
        if a == 0:
            build(group)
        wait_in(a, group)

        def sort(i, _):
            c = group * per_group + i
            sorted_[a, rows_of(c)] = jnp.dot(
                onehot[group, rows_of(i), :], rx[a, group], preferred_element_type=f32).astype(bf16)
            if a < 2:
                ycopy(a, 0, c).start()
                ycopy(a, 1, c).start()
            keep_copy(a, c).start()
            return 0

        lax.fori_loop(0, per_group, sort, 0)
        if a == 0 and group == 0:
            tables()
            table_copy.start()
            place_copy.start()
            destt_copy.start()
        if a < 2:
            def forward(i, _):
                c = group * per_group + i
                wait_y(a, 0, c)
                wait_y(a, 1, c)
                ycopy(a, 2, c).start()
                return 0

            lax.fori_loop(0, per_group, forward, 0)

    table_copy.wait()
    place_copy.wait()
    destt_copy.wait()

    def finish(c, _):
        for a in range(3):
            keep_copy(a, c).wait()
        for a in range(2):
            wait_y(a, 2, c)
            for kind in range(3):
                ycopy(a, kind, c).wait_send()
        return 0

    lax.fori_loop(0, CHUNKS, finish, 0)

    for a in range(3):
        for group in range(GROUPS):
            def sent(slot, _):
                a2a_copy(a, group, slot).wait_send()
                return 0

            lax.fori_loop(1 - group, SLOTS, sent, 0)


def gather_call(q, k, v, order, ext):
    any_ = pl.BlockSpec(memory_space=pl.ANY)
    vmem = pl.BlockSpec(memory_space=pltpu.VMEM)
    return pl.pallas_call(
        gather_kernel,
        out_shape=(
            jax.ShapeDtypeStruct((REPS, SPAN, DIM), bf16),
            jax.ShapeDtypeStruct((REPS, SPAN, DIM), bf16),
            jax.ShapeDtypeStruct((SPAN, DIM), bf16),
            jax.ShapeDtypeStruct((CLUSTERS, 128), i32),
            jax.ShapeDtypeStruct((REPS + 1, CLUSTERS, 128), i32),
            jax.ShapeDtypeStruct((LOCAL, HEADS), i32),
        ),
        in_specs=[any_, any_, any_, any_, vmem],
        out_specs=(any_,) * 6,
        scratch_shapes=[
            pltpu.VMEM((3, GROUPS, LIST, DIM), bf16),
            pltpu.VMEM((3, SPAN, DIM), bf16),
            pltpu.VMEM((GROUPS, LIST, LIST), bf16),
            pltpu.VMEM((128, 128), i32),
            pltpu.VMEM((128, 128), i32),
            pltpu.VMEM((128, 128), i32),
            pltpu.VMEM((4, 128, 128), f32),
            pltpu.VMEM((HEADS, LOCAL), i32),
            pltpu.VMEM((LOCAL, HEADS), i32),
            pltpu.VMEM((CLUSTERS, 128), i32),
            pltpu.VMEM((REPS + 1, CLUSTERS, 128), i32),
            pltpu.SemaphoreType.DMA((3, GROUPS, SLOTS)),
            pltpu.SemaphoreType.DMA((3, GROUPS, SLOTS)),
            pltpu.SemaphoreType.DMA((3,)),
            pltpu.SemaphoreType.DMA((128,)),
            pltpu.SemaphoreType.DMA((2, 3, CHUNKS)),
            pltpu.SemaphoreType.DMA((2, 3, CHUNKS)),
            pltpu.SemaphoreType.DMA((3, CHUNKS)),
            pltpu.SemaphoreType.DMA((3,)),
        ],
        compiler_params=pltpu.CompilerParams(
            collective_id=0, has_side_effects=True, vmem_limit_bytes=56 * 2**20),
        name="gather_sorted",
    )(q, k, v, order, ext)


GROUP = 8


def attend_kernel(table, list_ref, ext_ref, rep_ref, place_ref, kall, vall, qs, out, kc, vc, acc):
    rep = rep_ref[0]

    def span(c):
        return pl.ds(pl.multiple_of(c * CLUSTER, CLUSTER), CLUSTER)

    def half_span(c):
        return pl.ds(pl.multiple_of(c * DIM, DIM), DIM)

    def extent_of(c, r, group):
        return table[c, T_OFF + r * GROUPS + group], table[c, T_N + r * GROUPS + group]

    def picked(c, r, k, start):
        lane = iota((1, 128), 1)
        ats, shifts, lows, highs = [], [], [], []
        for group in range(GROUPS):
            off, n = extent_of(c, r, group)
            lo = (off // 16) * 16 + k * WINDOW
            at = jnp.minimum(lo, LIST - WINDOW)
            first = start + jnp.maximum(lo - off, 0)
            last = start + jnp.minimum(n, lo + WINDOW - off)
            ats.append(pl.multiple_of(at + group * LIST, 16))
            shifts.append(start + at - off - group * WINDOW)
            lows.append(first)
            highs.append(last)
            start = start + n
        is_first = lane < WINDOW
        place = lane + jnp.where(is_first, shifts[0], shifts[1])
        inside = (place >= jnp.where(is_first, lows[0], lows[1])) & (place < jnp.where(is_first, highs[0], highs[1]))
        return ats, jnp.where(inside, place, -1), start

    def first_windows(c, r):
        return [pl.multiple_of(table[c, r * GROUPS + g], 16) for g in range(GROUPS)]

    def windows_of(ref, ats, r):
        return [ref[r, pl.ds(at, WINDOW), :] for at in ats]

    def hot(place, rows):
        return jnp.where(iota((rows, 128), 0) == place, 1.0, 0.0).astype(bf16)

    def join(c, k):
        start = jnp.int32(0)
        hots, keys, vals = [], [], []
        for r in range(REPS):
            if k is None:
                ats, place = first_windows(c, r), place_ref[r, pl.ds(c, 1), :]
            else:
                ats, place, start = picked(c, r, k, start)
            hots.append(hot(place, CLUSTER))
            keys += windows_of(kall, ats, r)
            vals += windows_of(vall, ats, r)
        kv = jnp.concatenate([jnp.concatenate(keys, 0), jnp.concatenate(vals, 0)], 1)
        return jnp.dot(jnp.concatenate(hots, 1), kv, preferred_element_type=f32)

    def store(c, whole):
        kc[half_span(c), :] = whole[:, :DIM].T.astype(bf16)
        vc[span(c), :] = whole[:, DIM:].astype(bf16)

    def rounds(c, r):
        most = jnp.int32(0)
        for group in range(GROUPS):
            off, n = extent_of(c, r, group)
            most = jnp.maximum(most, off % 16 + n)
        return (most + WINDOW - 1) // WINDOW

    def compact(i, _):
        cs = [i * GROUP + u for u in range(GROUP)]
        for c in cs:
            store(c, join(c, None))
        for c in cs:
            @pl.when(table[c, T_OVER] > 0)
            def _():
                most = functools.reduce(jnp.maximum, [rounds(c, r) for r in range(REPS)])
                store(c, lax.fori_loop(0, most, lambda k, whole: whole + join(c, k),
                                       jnp.zeros((CLUSTER, 2 * DIM), f32)))
        return 0

    lax.fori_loop(0, CLUSTERS // GROUP, compact, 0)

    factor = DIM ** -0.5 * 1.4426950408889634

    def pick_queries(c, at, k):
        if k is None:
            ats, place = first_windows(c, rep), place_ref[REPS, pl.ds(c, 1), :]
        else:
            ats, place, _ = picked(c, rep, k, table[c, T_OFF_Q] - at)
        rows = [qs[pl.ds(a, WINDOW), :] for a in ats]
        return jnp.dot(hot(place, QROWS), jnp.concatenate(rows, 0), preferred_element_type=f32)

    def attend_rows(cs, k, size, slow):
        rows, live, blocks, tops, scores, queries = [], [], [], [], [], []
        for c in cs:
            off, n = table[c, T_OFF_Q], table[c, T_N_Q]
            if slow:
                lo = (off // 16) * 16 + k * QROWS
                at = jnp.minimum(lo, SPAN - QROWS)
            else:
                lo, at = 0, table[c, T_AT_Q]
            rows.append(pl.ds(pl.multiple_of(at, 16), QROWS))
            row = iota((QROWS, DIM), 0) + at
            live.append((row >= jnp.maximum(off, lo)) & (row < jnp.minimum(off + n, lo + QROWS)) if slow
                        else (row >= off) & (row < off + n))
            blocks.append([list_ref[jnp.where(j < ext_ref[c], j, 0), c] for j in range(size)])
            if slow:
                query = lax.fori_loop(0, rounds(c, rep), lambda i, q: q + pick_queries(c, at, i),
                                      jnp.zeros((QROWS, DIM), f32))
            else:
                query = pick_queries(c, at, None)
            queries.append(query.astype(bf16))
        for u in range(len(cs)):
            scores.append([jnp.dot(queries[u], kc[half_span(b), :], preferred_element_type=f32) for b in blocks[u]])
        for u in range(len(cs)):
            tops.append(jnp.max(functools.reduce(jnp.maximum, scores[u]), axis=1, keepdims=True))
        results = []
        for u, c in enumerate(cs):
            powers, sums = [], None
            for j in range(size):
                top = tops[u] if j == 0 else jnp.where(j < ext_ref[c], tops[u], jnp.inf)
                power = jnp.exp2((scores[u][j] - top) * factor)
                sums = power if sums is None else sums + power
                powers.append(power.astype(bf16))
            mixed = jnp.dot(jnp.concatenate(powers, 1), jnp.concatenate([vc[span(b), :] for b in blocks[u]], 0),
                            preferred_element_type=f32)
            results.append(mixed / jnp.sum(sums, axis=1, keepdims=True))
        for u in range(len(cs)):
            acc[rows[u], :] = jnp.where(live[u], results[u], acc[rows[u], :])

    def attend(g, _):
        cs = [table[g * GROUP + u, T_PERM] for u in range(GROUP)]
        size_most = ext_ref[cs[-1]]
        for size in range(1, 9):
            @pl.when(size_most == size)
            def _():
                attend_rows(cs, 0, size, False)
        for c in cs:
            def more(k, _):
                attend_rows([c], k, 8, True)
                return 0

            lax.fori_loop(jnp.where(table[c, T_OVER_Q] > 0, 0, 1), table[c, T_WINDOWS_Q], more, 0)
        return 0

    lax.fori_loop(0, CLUSTERS // GROUP, attend, 0)

    def finish(i, _):
        rows = pl.ds(pl.multiple_of(i * 512, 512), 512)
        out[rows, :] = acc[rows, :].astype(bf16)
        return 0

    lax.fori_loop(0, SPAN // 512, finish, 0)


def attend_call(table, listed, ext, rep, place, kall, vall, qs):
    smem = pl.BlockSpec(memory_space=pltpu.SMEM)
    vmem = pl.BlockSpec(memory_space=pltpu.VMEM)
    return pl.pallas_call(
        attend_kernel,
        out_shape=jax.ShapeDtypeStruct((SPAN, DIM), bf16),
        in_specs=[smem] * 4 + [vmem] * 4,
        out_specs=vmem,
        scratch_shapes=[
            pltpu.VMEM((CLUSTERS * DIM, CLUSTER), bf16),
            pltpu.VMEM((TOKENS, DIM), bf16),
            pltpu.VMEM((SPAN, DIM), f32),
        ],
        compiler_params=pltpu.CompilerParams(vmem_limit_bytes=56 * 2**20),
        name="attend",
    )(table, listed, ext, rep, place, kall, vall, qs)


HALF = HEADS // 2


def return_kernel(mixed_in, destt_in, out, mixed, destt_ref, partner_s, both_s, onehot, tx, swap_send, swap_recv,
                  send_sem, recv_sem, own_sem, in_sem):
    guide, me = lax.axis_index("guide"), lax.axis_index("seq")
    other = 1 - guide
    head_guide, head_col = me // HALF, me % HALF
    mixed_copy = pltpu.make_async_copy(mixed_in, mixed, in_sem.at[0])
    destt_copy = pltpu.make_async_copy(destt_in, destt_ref, in_sem.at[1])
    mixed_copy.start()
    destt_copy.start()

    barrier = pltpu.get_barrier_semaphore()
    pl.semaphore_signal(barrier, inc=1, device_id={"guide": other}, device_id_type=MESH)

    def greet(step, _):
        i = lax.rem(head_col + step, HALF)
        pl.semaphore_signal(barrier, inc=1, device_id={"guide": head_guide, "seq": guide * HALF + i},
                            device_id_type=MESH)
        return 0

    lax.fori_loop(1, HALF, greet, 0)

    @pl.when(head_guide != guide)
    def _():
        greet(0, 0)
        pl.semaphore_wait(barrier, HALF + 1)

    @pl.when(head_guide == guide)
    def _():
        pl.semaphore_wait(barrier, HALF)

    swap = pltpu.make_async_remote_copy(
        src_ref=mixed_in, dst_ref=partner_s, send_sem=swap_send, recv_sem=swap_recv,
        device_id={"guide": other}, device_id_type=MESH)
    swap.start()

    destt_copy.wait()
    destt = destt_ref[...]
    picked = jnp.where(guide == 0, destt[:, :HALF], destt[:, HALF:])
    for i in range(HALF):
        for c in range(SPAN // 512):
            onehot[i * LOCAL:(i + 1) * LOCAL, c * 512:(c + 1) * 512] = jnp.where(
                picked[:, i:i + 1] == iota((LOCAL, 512), 1) + c * 512, 1.0, 0.0).astype(bf16)
    mixed_copy.wait()
    swap.wait()

    def combine(c, _):
        rows = pl.ds(pl.multiple_of(c * 512, 512), 512)
        own = mixed[rows, :].astype(f32)
        far = partner_s[rows, :].astype(f32)
        conditioned = jnp.where(guide == 0, own, far)
        unconditioned = jnp.where(guide == 0, far, own)
        both_s[rows, :] = (unconditioned + GUIDE_SCALE * (conditioned - unconditioned)).astype(bf16)
        return 0

    lax.fori_loop(0, SPAN // 512, combine, 0)

    def place(col):
        return out.at[:, pl.ds(pl.multiple_of(col * DIM, DIM), DIM)]

    def send_copy(i):
        return pltpu.make_async_remote_copy(
            src_ref=tx.at[i], dst_ref=place(head_col), send_sem=send_sem.at[i],
            recv_sem=recv_sem.at[head_col],
            device_id={"guide": head_guide, "seq": guide * HALF + i}, device_id_type=MESH)

    def wait_copy(col):
        return pltpu.make_async_remote_copy(
            src_ref=tx.at[col], dst_ref=place(col), send_sem=send_sem.at[col],
            recv_sem=recv_sem.at[col], device_id={"guide": other}, device_id_type=MESH)

    own_copy = pltpu.make_async_copy(tx.at[head_col], place(head_col), own_sem)

    def restore(i):
        rows = pl.ds(pl.multiple_of(i * LOCAL, LOCAL), LOCAL)
        tx[i] = jnp.dot(onehot[rows, :], both_s[...], preferred_element_type=f32).astype(bf16)

    def step(j, _):
        i = lax.rem(head_col + j, HALF)
        restore(i)
        send_copy(i).start()
        return 0

    lax.fori_loop(1, HALF, step, 0)
    restore(head_col)

    @pl.when(head_guide == guide)
    def _():
        own_copy.start()

    @pl.when(head_guide != guide)
    def _():
        send_copy(head_col).start()

    def finish(j, _):
        i = lax.rem(head_col + j, HALF)
        send_copy(i).wait_send()
        wait_copy(i).wait_recv()
        return 0

    lax.fori_loop(1, HALF, finish, 0)

    @pl.when(head_guide == guide)
    def _():
        own_copy.wait()

    @pl.when(head_guide != guide)
    def _():
        send_copy(head_col).wait_send()
        wait_copy(head_col).wait_recv()


def return_call(mixed, destt):
    any_ = pl.BlockSpec(memory_space=pl.ANY)
    return pl.pallas_call(
        return_kernel,
        out_shape=jax.ShapeDtypeStruct((LOCAL, HALF * DIM), bf16),
        in_specs=[any_, any_],
        out_specs=any_,
        scratch_shapes=[
            pltpu.VMEM((SPAN, DIM), bf16),
            pltpu.VMEM((LOCAL, HEADS), i32),
            pltpu.VMEM((SPAN, DIM), bf16),
            pltpu.VMEM((SPAN, DIM), bf16),
            pltpu.VMEM((SPAN // 2, SPAN), bf16),
            pltpu.VMEM((HALF, LOCAL, DIM), bf16),
            pltpu.SemaphoreType.DMA,
            pltpu.SemaphoreType.DMA,
            pltpu.SemaphoreType.DMA((HALF,)),
            pltpu.SemaphoreType.DMA((HALF,)),
            pltpu.SemaphoreType.DMA,
            pltpu.SemaphoreType.DMA((2,)),
        ],
        compiler_params=pltpu.CompilerParams(
            collective_id=1, has_side_effects=True, vmem_limit_bytes=60 * 2**20),
        name="return_tokens",
    )(mixed, destt)


def on_device(queries, key_vectors, value_vectors, cluster_order, key_blocks, extents):
    kall, vall, qs, table, place, destt = gather_call(
        queries[0], key_vectors[0], value_vectors[0], cluster_order, extents)
    rep = lax.axis_index("rep").astype(i32).reshape(1)
    mixed = attend_call(table, key_blocks[0].T, extents[0], rep, place, kall, vall, qs)
    return return_call(mixed, destt)


def solution(mesh):
    placed = (
        P("guide", ("seq", "rep"), None),
        P("guide", ("seq", "rep"), None),
        P("guide", ("seq", "rep"), None),
        P("seq", None),
        P("seq", None, None),
        P("seq", None),
    )
    return jax.shard_map(
        on_device, mesh=mesh, in_specs=placed, out_specs=P(("seq", "rep"), "guide"), check_vma=False
    )
```

```python
import functools

import jax
import jax.numpy as jnp
from jax import lax
from jax.experimental import pallas as pl
from jax.experimental.pallas import tpu as pltpu
from jax.sharding import PartitionSpec as P

MESH = pl.DeviceIdType.MESH
CLUSTER = 256
GUIDE_SCALE = 5.0
HEADS = 32
SEQ_X, SEQ_Z = 4, 8
REPS = 4
TOKENS = 16384
DIM = 128
SPAN = TOKENS // REPS
LOCAL = 128
CLUSTERS = TOKENS // CLUSTER
CHUNK = 512
GROUPS = 2
SLOTS = HEADS // GROUPS
LIST = SPAN // GROUPS
WINDOW = 64
LISTS = REPS * GROUPS
T_OVER, T_OFF_Q, T_N_Q, T_AT_Q, T_OVER_Q, T_WINDOWS_Q, T_PERM = range(LISTS, LISTS + 7)
T_N, T_OFF = 2 * LISTS, 3 * LISTS
QROWS = 96
f32, bf16, i32 = jnp.float32, jnp.bfloat16, jnp.int32

NT = (((1,), (1,)), ((), ()))


def dot_nt(a, b):
    return lax.dot_general(a, b, NT, preferred_element_type=f32)


def iota(shape, dim):
    return lax.broadcasted_iota(i32, shape, dim)


def z_distance(group, dx, i):
    far = 4 * (dx // 2)
    if group == 0:
        return i + (i // 2) * 5 + (i // 3) * (far - 6)
    return i + 2 + (1 - (i + 2) // 3) * (4 - far)


def fill_tables(n, off, start, ext_row, rep, table, place):
    lane = iota((CLUSTERS, 128), 1)
    is_list = lane < LISTS
    at = jnp.minimum((off >> 4) << 4, LIST - WINDOW)
    lead = off - at
    over = jnp.where(is_list & (lead + n > WINDOW), 1, 0)
    own = is_list & ((lane >> 1) == rep)

    def total(a, hit):
        return jnp.sum(jnp.where(hit, a, 0).astype(f32), axis=1, keepdims=True).astype(i32)

    off_q, n_q = total(off, own), total(n, own)
    at_q = jnp.minimum((off_q >> 4) << 4, SPAN - QROWS)
    windows_q = ((off_q & 15) + n_q + QROWS - 1) // QROWS
    first = lane < WINDOW

    def both(a, r):
        return jnp.where(first, a[:, 2 * r:2 * r + 1], a[:, 2 * r + 1:2 * r + 2])

    chosen = jnp.full((CLUSTERS, 128), -1, i32)
    for r in range(REPS):
        start_r = both(start, r)
        spot = lane - jnp.where(first, 0, WINDOW) + start_r - both(lead, r)
        inside = (spot >= start_r) & (spot < start_r + both(n, r))
        place[r] = jnp.where(inside, spot, -1)
        queries = spot - start[:, 2 * r:2 * r + 1] + off_q - at_q
        chosen = jnp.where(rep == r, jnp.where(inside, queries, -1), chosen)
    place[REPS] = chosen

    c_row, c_col = iota((CLUSTERS, CLUSTERS), 1), iota((CLUSTERS, CLUSTERS), 0)
    diagonal = jnp.where(c_row == c_col, 1.0, 0.0).astype(bf16)
    ext_col = dot_nt(diagonal, jnp.broadcast_to(ext_row, (8, CLUSTERS)).astype(f32).astype(bf16))[:, 0:1].astype(i32)
    earlier = (ext_col < ext_row) | ((ext_col == ext_row) & (c_col < c_row))
    rank = jnp.sum(jnp.where(earlier, 1.0, 0.0), axis=0, keepdims=True).astype(i32)
    perm = jnp.sum(jnp.where(rank == c_col, c_row.astype(f32), 0.0), axis=1, keepdims=True).astype(i32)

    fields = jnp.where(is_list, at + (lane & 1) * LIST, 0)
    for field, value in ((T_OVER, total(over, is_list)), (T_OFF_Q, off_q), (T_N_Q, n_q), (T_AT_Q, at_q),
                         (T_OVER_Q, total(over, own)), (T_WINDOWS_Q, windows_q), (T_PERM, perm)):
        fields = jnp.where(lane == field, value, fields)
    for j in range(LISTS):
        fields = jnp.where(lane == T_N + j, n[:, j:j + 1], fields)
        fields = jnp.where(lane == T_OFF + j, off[:, j:j + 1], fields)
    table[...] = fields


def gather_kernel(q_in, k_in, v_in, order_in, ext_ref, kall, vall, qs, table_out, place_out, destt_out,
                  raw, raw_q, staged, staged_q, order_s, key_s, low_s, rank_s, dest_s, destt_s, table_s, place_s,
                  send_sem, recv_sem, own_sem, order_sem, ysend, yrecv, keep_sem, out_sem):
    me = lax.axis_index("seq")
    rep = lax.axis_index("rep")
    x, z = me // SEQ_Z, me % SEQ_Z
    right, left = lax.rem(rep + 1, REPS), lax.rem(rep + REPS - 1, REPS)
    far = lax.rem(rep + 2, REPS)
    ins = (k_in, v_in, q_in)

    def at_distance(group, slot, sign):
        dx = slot // 4
        dz = z_distance(group, dx, slot % 4)
        return lax.rem(x + sign * dx + SEQ_X, SEQ_X) * SEQ_Z + lax.rem(z + sign * dz + SEQ_Z, SEQ_Z)

    def order_copy(u):
        return pltpu.make_async_copy(
            order_in.at[:, pl.ds(pl.multiple_of(u * 128, 128), 128)], order_s.at[pl.ds(u, 1), :], order_sem.at[u])

    def fetch(u, _):
        order_copy(u).start()
        return 0

    lax.fori_loop(0, 128, fetch, 0)

    barrier = pltpu.get_barrier_semaphore()
    for group in range(GROUPS):
        def greet(slot, _):
            pl.semaphore_signal(barrier, inc=1, device_id={"seq": at_distance(group, slot, 1)}, device_id_type=MESH)
            return 0

        lax.fori_loop(1 - group, SLOTS, greet, 0)
    pl.semaphore_signal(barrier, inc=1, device_id={"rep": right}, device_id_type=MESH)
    pl.semaphore_signal(barrier, inc=1, device_id={"rep": left}, device_id_type=MESH)
    pl.semaphore_wait(barrier, HEADS - 1 + 2)

    def landing(a, group, slot):
        rows = pl.ds(pl.multiple_of(slot * LOCAL, LOCAL), LOCAL)
        return raw.at[a, rep, group, rows] if a < 2 else raw_q.at[group, rows]

    def a2a_copy(a, group, slot):
        peer = at_distance(group, slot, 1)
        return pltpu.make_async_remote_copy(
            src_ref=ins[a].at[:, pl.ds(pl.multiple_of(peer * DIM, DIM), DIM)],
            dst_ref=landing(a, group, slot),
            send_sem=send_sem.at[a, group, slot], recv_sem=recv_sem.at[a, group, slot],
            device_id={"seq": peer}, device_id_type=MESH)

    def own_copy(a):
        return pltpu.make_async_copy(
            ins[a].at[:, pl.ds(pl.multiple_of(me * DIM, DIM), DIM)], landing(a, 0, 0), own_sem.at[a])

    units = ((0, 0), (1, 0), (0, 1), (1, 1), (2, 0), (2, 1))
    for a, group in units:
        if group == 0:
            own_copy(a).start()

        def send(slot, _):
            a2a_copy(a, group, slot).start()
            return 0

        lax.fori_loop(1 - group, SLOTS, send, 0)

    def rows_of(c):
        return pl.ds(pl.multiple_of(c * CHUNK, CHUNK), CHUNK)

    def ycopy(a, kind, group, c):
        if kind == 0:
            slot, to = rep, right
        elif kind == 1:
            slot, to = rep, left
        else:
            even = lax.rem(c, 2) == 0
            slot = jnp.where(even, left, right)
            to = jnp.where(even, right, left)
        piece = raw.at[a, slot, group, rows_of(c)]
        return pltpu.make_async_remote_copy(
            src_ref=piece, dst_ref=piece,
            send_sem=ysend.at[a, kind, group, c], recv_sem=yrecv.at[a, kind, group, c],
            device_id={"rep": to}, device_id_type=MESH)

    def wait_y(a, kind, group, c):
        piece = raw.at[a, (left, right, far)[kind], group, rows_of(c)]
        pltpu.make_async_remote_copy(
            src_ref=piece, dst_ref=piece,
            send_sem=ysend.at[a, kind, group, c], recv_sem=yrecv.at[a, kind, group, c],
            device_id={"rep": right}, device_id_type=MESH).wait_recv()

    def wait_slot(a, group, slot, _):
        a2a_copy(a, group, slot).wait_recv()
        return 0

    per_chunk, chunks = CHUNK // LOCAL, LIST // CHUNK

    def pass_on(a, group):
        def one(c, _):
            ycopy(a, 0, group, c).start()
            ycopy(a, 1, group, c).start()
            return 0

        def arrived(c, _):
            lax.fori_loop(0, per_chunk, lambda i, _: wait_slot(a, group, c * per_chunk + i, _), 0)
            return one(c, _)

        if group == 0:
            lax.fori_loop(1, per_chunk, lambda i, _: wait_slot(a, group, i, _), 0)
            own_copy(a).wait()
            one(0, 0)
        lax.fori_loop(1 - group, chunks, arrived, 0)

    def forward(a, group):
        def one(c, _):
            wait_y(a, 0, group, c)
            wait_y(a, 1, group, c)
            ycopy(a, 2, group, c).start()
            return 0

        lax.fori_loop(0, chunks, one, 0)

    def settle(a, group):
        def one(c, _):
            wait_y(a, 2, group, c)
            return 0

        lax.fori_loop(0, chunks, one, 0)

    pass_on(0, 0)

    def fetched(u, _):
        order_copy(u).wait()
        return 0

    lax.fori_loop(0, 128, fetched, 0)

    order = order_s[...]
    block = order >> 7
    owner = block & (REPS - 1)
    away_x = (x - (block >> 5)) & (SEQ_X - 1)
    away_z = (z - (block >> 2)) & (SEQ_Z - 1)
    near = (away_z == 0) | (away_z == 1) | (away_z == 7) | (away_z == 2 + 4 * (away_x >> 1))
    second = jnp.where(near, 0, 1)
    mine = owner == rep
    rows, cols = iota((128, 128), 0), iota((128, 128), 1)
    as_mask = lambda hit: jnp.where(hit, 1.0, 0.0).astype(bf16)
    product = lambda a, b: jnp.dot(a, b, preferred_element_type=f32)
    upper, lower = as_mask(rows < cols), as_mask(cols < rows)
    to_cluster, past_cluster = as_mask(cols < (rows >> 1) * 2), as_mask(cols < (rows >> 1) * 2 + 2)
    ones = jnp.ones((128, 128), bf16)
    rank = jnp.zeros((128, 128), f32)
    for r in range(REPS):
        for group in range(GROUPS):
            hit = (owner == r) & (second == group)
            present = as_mask(hit)
            totals = product(present, ones).astype(bf16)
            rank = jnp.where(hit, product(present, upper) + product(lower, totals), rank)
    own_totals = [product(as_mask(mine & (second == group)), ones).astype(bf16) for group in range(GROUPS)]
    whole = rank + jnp.where(second == 0, product(to_cluster, own_totals[1]), product(past_cluster, own_totals[0]))
    rank_hi, whole_hi = jnp.floor(rank * (1.0 / 64.0)), jnp.floor(whole * (1.0 / 64.0))
    key_s[0] = block
    key_s[1] = jnp.where(mine, block >> 2, -1)
    low_s[...] = order & (LOCAL - 1)
    rank_s[0] = rank_hi
    rank_s[1] = rank - 64.0 * rank_hi
    rank_s[2] = whole_hi
    rank_s[3] = whole - 64.0 * whole_hi

    def accumulate(step, carry):
        d, dt = carry
        parts, bs = [[], [], [], []], []
        base = pl.multiple_of(step * 32, 32)
        keys = [key_s[i, pl.ds(base, 32), :] for i in range(2)]
        low = low_s[pl.ds(base, 32), :]
        values = [rank_s[i, pl.ds(base, 32), :] for i in range(4)]
        for j in range(32):
            hit_all = iota((128, 128), 0) == keys[0][j:j + 1]
            hit_own = iota((HEADS, 128), 0) == keys[1][j:j + 1]
            for i in range(4):
                parts[i].append(jnp.where(hit_all if i < 2 else hit_own, values[i][j:j + 1], 0.0).astype(bf16))
            bs.append(as_mask(iota((128, 128), 0) == low[j:j + 1]))
        parts = [jnp.concatenate(p, 1) for p in parts]
        right_m = jnp.concatenate(bs, 1)
        d = d + dot_nt(jnp.concatenate(parts[:2], 0), right_m)
        dt = dt + dot_nt(right_m, jnp.concatenate(parts[2:], 0))
        return d, dt

    d, dt = lax.fori_loop(0, 4, accumulate, (jnp.zeros((256, 128), f32), jnp.zeros((128, 2 * HEADS), f32)))
    dest_s[...] = (64.0 * d[:128] + d[128:]).astype(i32)
    destt_s[...] = (64.0 * dt[:, :HEADS] + dt[:, HEADS:]).astype(i32)

    def tables():
        listed = jnp.zeros((128, 128), f32)
        for r in range(REPS):
            for group in range(GROUPS):
                listed = listed + product(
                    as_mask((owner == r) & (second == group)), as_mask(cols == r * GROUPS + group))
        pair = as_mask((iota((CLUSTERS, 128), 1) >> 1) == iota((CLUSTERS, 128), 0))
        counts = product(pair, listed.astype(bf16)).astype(bf16)
        before = as_mask(iota((CLUSTERS, CLUSTERS), 1) < iota((CLUSTERS, CLUSTERS), 0))
        offsets = product(before, counts)
        starts = product(counts, upper)
        fill_tables(counts.astype(f32).astype(i32), offsets.astype(i32), starts.astype(i32), ext_ref[...], rep,
                    table_s, place_s)

    def sort(r, group, is_query):
        lines = [dest_s[pl.ds(at_distance(group, slot, -1) * REPS + r, 1), :] for slot in range(SLOTS)]

        def some(c, _):
            base = pl.multiple_of(c * CHUNK, CHUNK)
            hot = jnp.concatenate([as_mask(iota((CHUNK, 128), 0) + base == line) for line in lines], 1)
            rows = pl.ds(pl.multiple_of(group * LIST + base, CHUNK), CHUNK)
            if is_query:
                staged_q[rows, :] = product(hot, raw_q[group]).astype(bf16)
            else:
                both = product(hot, jnp.concatenate([raw[0, r, group], raw[1, r, group]], 1)).astype(bf16)
                staged[0, r, rows, :] = both[:, :DIM]
                staged[1, r, rows, :] = both[:, DIM:]
            return 0

        lax.fori_loop(0, LIST // CHUNK, some, 0)
        for copy in keep_copies(r, group, is_query):
            copy.start()

    def keep_copies(r, group, is_query):
        rows = pl.ds(group * LIST, LIST)
        if is_query:
            return [pltpu.make_async_copy(staged_q.at[rows], qs.at[rows], keep_sem.at[2, group, 0])]
        return [pltpu.make_async_copy(staged.at[a, r, rows], out.at[r, rows], keep_sem.at[a, group, r])
                for a, out in enumerate((kall, vall))]

    table_copy = pltpu.make_async_copy(table_s, table_out, out_sem.at[0])
    destt_copy = pltpu.make_async_copy(destt_s, destt_out, out_sem.at[1])
    place_copy = pltpu.make_async_copy(place_s, place_out, out_sem.at[2])
    pass_on(1, 0)
    forward(0, 0)
    tables()
    table_copy.start()
    destt_copy.start()
    place_copy.start()
    sort(rep, 0, False)
    pass_on(0, 1)
    forward(1, 0)
    sort(left, 0, False)
    sort(right, 0, False)
    pass_on(1, 1)
    forward(0, 1)
    settle(0, 0)
    settle(1, 0)
    sort(far, 0, False)
    sort(rep, 1, False)
    forward(1, 1)
    sort(left, 1, False)
    sort(right, 1, False)
    for group in range(GROUPS):
        lax.fori_loop(1 - group, SLOTS, lambda slot, _: wait_slot(2, group, slot, _), 0)
        if group == 0:
            own_copy(2).wait()
        sort(rep, group, True)
    settle(0, 1)
    settle(1, 1)
    sort(far, 1, False)

    table_copy.wait()
    destt_copy.wait()
    place_copy.wait()
    for group in range(GROUPS):
        for r in range(REPS):
            for copy in keep_copies(r, group, False):
                copy.wait()
        keep_copies(rep, group, True)[0].wait()

        def finish(c, _):
            for a in range(2):
                for kind in range(3):
                    ycopy(a, kind, group, c).wait_send()
            return 0

        lax.fori_loop(0, chunks, finish, 0)
        for a in range(3):
            def sent(slot, _):
                a2a_copy(a, group, slot).wait_send()
                return 0

            lax.fori_loop(1 - group, SLOTS, sent, 0)


def gather_call(q, k, v, order, ext):
    any_ = pl.BlockSpec(memory_space=pl.ANY)
    vmem = pl.BlockSpec(memory_space=pltpu.VMEM)
    return pl.pallas_call(
        gather_kernel,
        out_shape=(
            jax.ShapeDtypeStruct((REPS, SPAN, DIM), bf16),
            jax.ShapeDtypeStruct((REPS, SPAN, DIM), bf16),
            jax.ShapeDtypeStruct((SPAN, DIM), bf16),
            jax.ShapeDtypeStruct((CLUSTERS, 128), i32),
            jax.ShapeDtypeStruct((REPS + 1, CLUSTERS, 128), i32),
            jax.ShapeDtypeStruct((LOCAL, HEADS), i32),
        ),
        in_specs=[any_, any_, any_, any_, vmem],
        out_specs=(any_,) * 6,
        scratch_shapes=[
            pltpu.VMEM((2, REPS, GROUPS, LIST, DIM), bf16),
            pltpu.VMEM((GROUPS, LIST, DIM), bf16),
            pltpu.VMEM((2, REPS, SPAN, DIM), bf16),
            pltpu.VMEM((SPAN, DIM), bf16),
            pltpu.VMEM((128, 128), i32),
            pltpu.VMEM((2, 128, 128), i32),
            pltpu.VMEM((128, 128), i32),
            pltpu.VMEM((4, 128, 128), f32),
            pltpu.VMEM((128, 128), i32),
            pltpu.VMEM((LOCAL, HEADS), i32),
            pltpu.VMEM((CLUSTERS, 128), i32),
            pltpu.VMEM((REPS + 1, CLUSTERS, 128), i32),
            pltpu.SemaphoreType.DMA((3, GROUPS, SLOTS)),
            pltpu.SemaphoreType.DMA((3, GROUPS, SLOTS)),
            pltpu.SemaphoreType.DMA((3,)),
            pltpu.SemaphoreType.DMA((128,)),
            pltpu.SemaphoreType.DMA((2, 3, GROUPS, LIST // CHUNK)),
            pltpu.SemaphoreType.DMA((2, 3, GROUPS, LIST // CHUNK)),
            pltpu.SemaphoreType.DMA((3, GROUPS, REPS)),
            pltpu.SemaphoreType.DMA((3,)),
        ],
        compiler_params=pltpu.CompilerParams(
            collective_id=0, has_side_effects=True, vmem_limit_bytes=56 * 2**20),
        name="gather_sorted",
    )(q, k, v, order, ext)


GROUP = 8


def attend_kernel(table, list_ref, ext_ref, rep_ref, place_ref, kall, vall, qs, out, kc, vc, acc):
    rep = rep_ref[0]

    def span(c):
        return pl.ds(pl.multiple_of(c * CLUSTER, CLUSTER), CLUSTER)

    def half_span(c):
        return pl.ds(pl.multiple_of(c * DIM, DIM), DIM)

    def extent_of(c, r, group):
        return table[c, T_OFF + r * GROUPS + group], table[c, T_N + r * GROUPS + group]

    def picked(c, r, k, start):
        lane = iota((1, 128), 1)
        ats, shifts, lows, highs = [], [], [], []
        for group in range(GROUPS):
            off, n = extent_of(c, r, group)
            lo = (off // 16) * 16 + k * WINDOW
            at = jnp.minimum(lo, LIST - WINDOW)
            first = start + jnp.maximum(lo - off, 0)
            last = start + jnp.minimum(n, lo + WINDOW - off)
            ats.append(pl.multiple_of(at + group * LIST, 16))
            shifts.append(start + at - off - group * WINDOW)
            lows.append(first)
            highs.append(last)
            start = start + n
        is_first = lane < WINDOW
        place = lane + jnp.where(is_first, shifts[0], shifts[1])
        inside = (place >= jnp.where(is_first, lows[0], lows[1])) & (place < jnp.where(is_first, highs[0], highs[1]))
        return ats, jnp.where(inside, place, -1), start

    def first_windows(c, r):
        return [pl.multiple_of(table[c, r * GROUPS + g], 16) for g in range(GROUPS)]

    def windows_of(ref, ats, r):
        return [ref[r, pl.ds(at, WINDOW), :] for at in ats]

    def hot(place, rows):
        return jnp.where(iota((rows, 128), 0) == place, 1.0, 0.0).astype(bf16)

    def join(c, k):
        start = jnp.int32(0)
        hots, keys, vals = [], [], []
        for r in range(REPS):
            if k is None:
                ats, place = first_windows(c, r), place_ref[r, pl.ds(c, 1), :]
            else:
                ats, place, start = picked(c, r, k, start)
            hots.append(hot(place, CLUSTER))
            keys += windows_of(kall, ats, r)
            vals += windows_of(vall, ats, r)
        kv = jnp.concatenate([jnp.concatenate(keys, 0), jnp.concatenate(vals, 0)], 1)
        return jnp.dot(jnp.concatenate(hots, 1), kv, preferred_element_type=f32)

    def store(c, whole):
        kc[half_span(c), :] = whole[:, :DIM].T.astype(bf16)
        vc[span(c), :] = whole[:, DIM:].astype(bf16)

    def rounds(c, r):
        most = jnp.int32(0)
        for group in range(GROUPS):
            off, n = extent_of(c, r, group)
            most = jnp.maximum(most, off % 16 + n)
        return (most + WINDOW - 1) // WINDOW

    def compact(i, _):
        cs = [i * GROUP + u for u in range(GROUP)]
        for c in cs:
            store(c, join(c, None))
        for c in cs:
            @pl.when(table[c, T_OVER] > 0)
            def _():
                most = functools.reduce(jnp.maximum, [rounds(c, r) for r in range(REPS)])
                store(c, lax.fori_loop(0, most, lambda k, whole: whole + join(c, k),
                                       jnp.zeros((CLUSTER, 2 * DIM), f32)))
        return 0

    lax.fori_loop(0, CLUSTERS // GROUP, compact, 0)

    factor = DIM ** -0.5 * 1.4426950408889634

    def pick_queries(c, at, k):
        if k is None:
            ats, place = first_windows(c, rep), place_ref[REPS, pl.ds(c, 1), :]
        else:
            ats, place, _ = picked(c, rep, k, table[c, T_OFF_Q] - at)
        rows = [qs[pl.ds(a, WINDOW), :] for a in ats]
        return jnp.dot(hot(place, QROWS), jnp.concatenate(rows, 0), preferred_element_type=f32)

    def attend_rows(cs, k, size, slow):
        rows, live, blocks, tops, scores, queries = [], [], [], [], [], []
        for c in cs:
            off, n = table[c, T_OFF_Q], table[c, T_N_Q]
            if slow:
                lo = (off // 16) * 16 + k * QROWS
                at = jnp.minimum(lo, SPAN - QROWS)
            else:
                lo, at = 0, table[c, T_AT_Q]
            rows.append(pl.ds(pl.multiple_of(at, 16), QROWS))
            row = iota((QROWS, DIM), 0) + at
            live.append((row >= jnp.maximum(off, lo)) & (row < jnp.minimum(off + n, lo + QROWS)) if slow
                        else (row >= off) & (row < off + n))
            blocks.append([list_ref[jnp.where(j < ext_ref[c], j, 0), c] for j in range(size)])
            if slow:
                query = lax.fori_loop(0, rounds(c, rep), lambda i, q: q + pick_queries(c, at, i),
                                      jnp.zeros((QROWS, DIM), f32))
            else:
                query = pick_queries(c, at, None)
            queries.append(query.astype(bf16))
        for u in range(len(cs)):
            scores.append([jnp.dot(queries[u], kc[half_span(b), :], preferred_element_type=f32) for b in blocks[u]])
        for u in range(len(cs)):
            tops.append(jnp.max(functools.reduce(jnp.maximum, scores[u]), axis=1, keepdims=True))
        results = []
        for u, c in enumerate(cs):
            powers, sums = [], None
            for j in range(size):
                top = tops[u] if j == 0 else jnp.where(j < ext_ref[c], tops[u], jnp.inf)
                power = jnp.exp2((scores[u][j] - top) * factor)
                sums = power if sums is None else sums + power
                powers.append(power.astype(bf16))
            mixed = jnp.dot(jnp.concatenate(powers, 1), jnp.concatenate([vc[span(b), :] for b in blocks[u]], 0),
                            preferred_element_type=f32)
            results.append(mixed / jnp.sum(sums, axis=1, keepdims=True))
        for u in range(len(cs)):
            acc[rows[u], :] = jnp.where(live[u], results[u], acc[rows[u], :])

    def attend(g, _):
        cs = [table[g * GROUP + u, T_PERM] for u in range(GROUP)]
        size_most = ext_ref[cs[-1]]
        for size in range(1, 9):
            @pl.when(size_most == size)
            def _():
                attend_rows(cs, 0, size, False)
        for c in cs:
            def more(k, _):
                attend_rows([c], k, 8, True)
                return 0

            lax.fori_loop(jnp.where(table[c, T_OVER_Q] > 0, 0, 1), table[c, T_WINDOWS_Q], more, 0)
        return 0

    lax.fori_loop(0, CLUSTERS // GROUP, attend, 0)

    def finish(i, _):
        rows = pl.ds(pl.multiple_of(i * 512, 512), 512)
        out[rows, :] = acc[rows, :].astype(bf16)
        return 0

    lax.fori_loop(0, SPAN // 512, finish, 0)


def attend_call(table, listed, ext, rep, place, kall, vall, qs):
    smem = pl.BlockSpec(memory_space=pltpu.SMEM)
    vmem = pl.BlockSpec(memory_space=pltpu.VMEM)
    return pl.pallas_call(
        attend_kernel,
        out_shape=jax.ShapeDtypeStruct((SPAN, DIM), bf16),
        in_specs=[smem] * 4 + [vmem] * 4,
        out_specs=vmem,
        scratch_shapes=[
            pltpu.VMEM((CLUSTERS * DIM, CLUSTER), bf16),
            pltpu.VMEM((TOKENS, DIM), bf16),
            pltpu.VMEM((SPAN, DIM), f32),
        ],
        compiler_params=pltpu.CompilerParams(vmem_limit_bytes=56 * 2**20),
        name="attend",
    )(table, listed, ext, rep, place, kall, vall, qs)


HALF = HEADS // 2


def return_kernel(mixed_in, destt_in, out, mixed, destt_ref, partner_s, both_s, onehot, tx, swap_send, swap_recv,
                  send_sem, recv_sem, own_sem, in_sem):
    guide, me = lax.axis_index("guide"), lax.axis_index("seq")
    other = 1 - guide
    head_guide, head_col = me // HALF, me % HALF
    mixed_copy = pltpu.make_async_copy(mixed_in, mixed, in_sem.at[0])
    destt_copy = pltpu.make_async_copy(destt_in, destt_ref, in_sem.at[1])
    mixed_copy.start()
    destt_copy.start()

    barrier = pltpu.get_barrier_semaphore()
    pl.semaphore_signal(barrier, inc=1, device_id={"guide": other}, device_id_type=MESH)

    def greet(step, _):
        i = lax.rem(head_col + step, HALF)
        pl.semaphore_signal(barrier, inc=1, device_id={"guide": head_guide, "seq": guide * HALF + i},
                            device_id_type=MESH)
        return 0

    lax.fori_loop(1, HALF, greet, 0)

    @pl.when(head_guide != guide)
    def _():
        greet(0, 0)
        pl.semaphore_wait(barrier, HALF + 1)

    @pl.when(head_guide == guide)
    def _():
        pl.semaphore_wait(barrier, HALF)

    swap = pltpu.make_async_remote_copy(
        src_ref=mixed_in, dst_ref=partner_s, send_sem=swap_send, recv_sem=swap_recv,
        device_id={"guide": other}, device_id_type=MESH)
    swap.start()

    destt_copy.wait()
    destt = destt_ref[...]
    picked = jnp.where(guide == 0, destt[:, :HALF], destt[:, HALF:])
    for i in range(HALF):
        for c in range(SPAN // 512):
            onehot[i * LOCAL:(i + 1) * LOCAL, c * 512:(c + 1) * 512] = jnp.where(
                picked[:, i:i + 1] == iota((LOCAL, 512), 1) + c * 512, 1.0, 0.0).astype(bf16)
    mixed_copy.wait()
    swap.wait()

    def combine(c, _):
        rows = pl.ds(pl.multiple_of(c * 512, 512), 512)
        own = mixed[rows, :].astype(f32)
        far = partner_s[rows, :].astype(f32)
        conditioned = jnp.where(guide == 0, own, far)
        unconditioned = jnp.where(guide == 0, far, own)
        both_s[rows, :] = (unconditioned + GUIDE_SCALE * (conditioned - unconditioned)).astype(bf16)
        return 0

    lax.fori_loop(0, SPAN // 512, combine, 0)

    def place(col):
        return out.at[:, pl.ds(pl.multiple_of(col * DIM, DIM), DIM)]

    def send_copy(i):
        return pltpu.make_async_remote_copy(
            src_ref=tx.at[i], dst_ref=place(head_col), send_sem=send_sem.at[i],
            recv_sem=recv_sem.at[head_col],
            device_id={"guide": head_guide, "seq": guide * HALF + i}, device_id_type=MESH)

    def wait_copy(col):
        return pltpu.make_async_remote_copy(
            src_ref=tx.at[col], dst_ref=place(col), send_sem=send_sem.at[col],
            recv_sem=recv_sem.at[col], device_id={"guide": other}, device_id_type=MESH)

    own_copy = pltpu.make_async_copy(tx.at[head_col], place(head_col), own_sem)

    def restore(i):
        rows = pl.ds(pl.multiple_of(i * LOCAL, LOCAL), LOCAL)
        tx[i] = jnp.dot(onehot[rows, :], both_s[...], preferred_element_type=f32).astype(bf16)

    def step(j, _):
        i = lax.rem(head_col + j, HALF)
        restore(i)
        send_copy(i).start()
        return 0

    lax.fori_loop(1, HALF, step, 0)
    restore(head_col)

    @pl.when(head_guide == guide)
    def _():
        own_copy.start()

    @pl.when(head_guide != guide)
    def _():
        send_copy(head_col).start()

    def finish(j, _):
        i = lax.rem(head_col + j, HALF)
        send_copy(i).wait_send()
        wait_copy(i).wait_recv()
        return 0

    lax.fori_loop(1, HALF, finish, 0)

    @pl.when(head_guide == guide)
    def _():
        own_copy.wait()

    @pl.when(head_guide != guide)
    def _():
        send_copy(head_col).wait_send()
        wait_copy(head_col).wait_recv()


def return_call(mixed, destt):
    any_ = pl.BlockSpec(memory_space=pl.ANY)
    return pl.pallas_call(
        return_kernel,
        out_shape=jax.ShapeDtypeStruct((LOCAL, HALF * DIM), bf16),
        in_specs=[any_, any_],
        out_specs=any_,
        scratch_shapes=[
            pltpu.VMEM((SPAN, DIM), bf16),
            pltpu.VMEM((LOCAL, HEADS), i32),
            pltpu.VMEM((SPAN, DIM), bf16),
            pltpu.VMEM((SPAN, DIM), bf16),
            pltpu.VMEM((SPAN // 2, SPAN), bf16),
            pltpu.VMEM((HALF, LOCAL, DIM), bf16),
            pltpu.SemaphoreType.DMA,
            pltpu.SemaphoreType.DMA,
            pltpu.SemaphoreType.DMA((HALF,)),
            pltpu.SemaphoreType.DMA((HALF,)),
            pltpu.SemaphoreType.DMA,
            pltpu.SemaphoreType.DMA((2,)),
        ],
        compiler_params=pltpu.CompilerParams(
            collective_id=1, has_side_effects=True, vmem_limit_bytes=60 * 2**20),
        name="return_tokens",
    )(mixed, destt)


def on_device(queries, key_vectors, value_vectors, cluster_order, key_blocks, extents):
    kall, vall, qs, table, place, destt = gather_call(
        queries[0], key_vectors[0], value_vectors[0], cluster_order, extents)
    rep = lax.axis_index("rep").astype(i32).reshape(1)
    mixed = attend_call(table, key_blocks[0].T, extents[0], rep, place, kall, vall, qs)
    return return_call(mixed, destt)


def solution(mesh):
    placed = (
        P("guide", ("seq", "rep"), None),
        P("guide", ("seq", "rep"), None),
        P("guide", ("seq", "rep"), None),
        P("seq", None),
        P("seq", None, None),
        P("seq", None),
    )
    return jax.shard_map(
        on_device, mesh=mesh, in_specs=placed, out_specs=P(("seq", "rep"), "guide"), check_vma=False
    )
```
